256 devices in a mesh: cuts: 4 (over z_hi, core), member: 16 (over y, z_lo), grid: 4 (over x).
Axes of the slice: x: 4, y: 4, z: 8 (z_hi: 2, z_lo: 4; z = z_hi * 4 + z_lo), core: 2. Of those that a mesh axis runs over, the one named last changes fastest.
Arguments:
- hidden: bfloat16 [4, 16, 8192, 1024], P('cuts', 'member', 'grid'), may hold values from -6 to 6
- noise_seeds: int32 [16], P('member'), may hold values from 0 to 63
- noise_table: float32 [64, 1024], replicated, may hold values from -4 to 4
- inner_weight: bfloat16 [1024, 1024], replicated, may hold values from -0.1875 to 0.1875
- inner_bias: float32 [1024], replicated, may hold values from -3 to 3
- output_weight: bfloat16 [100, 1024], replicated, may hold values from -0.1875 to 0.1875
- output_bias: float32 [100], replicated, may hold values from -3 to 3
- state_bank: float32 [8, 100, 4, 16, 128], P(None, None, 'grid', 'member'), may hold values from -6 to 6
- ic_index: int32 [4], P('cuts'), may hold values from 0 to 7
- target_index: int32 [4], P('cuts'), may hold values from 0 to 7
- area_weight: float32 [4, 16, 128], P('grid', 'member'), may hold values from 0.1 to 1
Outputs:
- inner_weight_grad: float32 [1024, 1024], replicated
- inner_bias_grad: float32 [1024], replicated
- output_weight_grad: float32 [100, 1024], replicated
- output_bias_grad: float32 [100], replicated
- loss: float32 [], replicated
The draws below stay inside these ranges and needn't reach their ends.
All inputs are finite; a program needn't handle non-finite values.
Results may differ from the reference program's by a relative error of at most 0.0037.
Values may be sent and summed in bfloat16 or wider, within the bound.
A program may use at most 128 MiB of HBM per device.

```python
import math
import jax
import jax.numpy as jnp
from jax import lax

HID = 1024
VARS = 100
MEMBERS = 16
SEEDS = 64
BANK = 8
SAMPLES = 4
PTS_SUB = 128
POINTS = 8192
GBLOCKS = 4
MBLOCKS = 16


def plant(entries, rng, smallest, high):
    longest = entries.shape.index(max(entries.shape))
    spots = []
    for shift in (0, 1):
        where = [jax.random.randint(jax.random.fold_in(rng, axis), (), 0, length) for axis, length in enumerate(entries.shape)]
        where[longest] = (where[longest] + shift) % entries.shape[longest]
        spots.append(tuple(where))
    return entries.at[spots[0]].set(smallest).at[spots[1]].set(high)


def block_scale(rng, shape, split, least, high):
    def one(position, parts):
        steps = jax.random.uniform(jax.random.fold_in(jax.random.fold_in(rng, 6), position), (parts,), jnp.float32, least / len(split), high / len(split))
        return jnp.repeat(jnp.exp(steps), shape[position] // parts).reshape((-1,) + (1,) * (len(shape) - position - 1))

    level = one(*split[0])
    for cut in split[1:]:
        level = level * one(*cut)
    return level


def bell_draw(key, extent, deviation, reach, split=(), held_as=jnp.bfloat16):
    array = jax.random.normal(key, extent, jnp.float32) * deviation
    if len(split) > 0:
        array = block_scale(key, extent, split, -0.22, 0.18) * array
    return jnp.clip(array, min=-reach, max=reach).astype(held_as)


def setup_inputs(seed: int = 0) -> dict:
    splits = jax.random.split(jax.random.key(seed), 12)
    hidden = bell_draw(splits[0], (SAMPLES, MEMBERS, POINTS, HID), 1.0, 6.0, ((0, 4), (1, 16), (2, 4)))
    noise_seeds = plant(jax.random.randint(splits[1], (MEMBERS,), 0, SEEDS), jax.random.fold_in(splits[1], 1), 0, SEEDS - 1).astype(jnp.int32)
    noise_table = bell_draw(splits[2], (SEEDS, HID), 0.5, 4.0, (), jnp.float32)
    inner_weight = bell_draw(splits[3], (HID, HID), HID ** -0.5, 0.1875)
    inner_bias = bell_draw(splits[4], (HID,), 0.5, 3.0, (), jnp.float32)
    output_weight = bell_draw(splits[5], (VARS, HID), HID ** -0.5, 0.1875)
    output_bias = bell_draw(splits[6], (VARS,), 0.5, 3.0, (), jnp.float32)
    state_bank = bell_draw(splits[7], (BANK, VARS, GBLOCKS, MBLOCKS, PTS_SUB), 1.0, 6.0, ((2, 4), (3, 16)), jnp.float32)
    ic_index = plant(jax.random.randint(splits[8], (SAMPLES,), 0, BANK), jax.random.fold_in(splits[8], 1), 0, BANK - 1).astype(jnp.int32)
    target_index = plant(jax.random.randint(splits[9], (SAMPLES,), 0, BANK), jax.random.fold_in(splits[9], 1), 0, BANK - 1).astype(jnp.int32)
    area_weight = jnp.clip(jnp.exp(math.log(1.0) - 2.3025851 * jax.random.uniform(splits[10], (GBLOCKS, MBLOCKS, PTS_SUB), jnp.float32) ** block_scale(splits[10], (GBLOCKS, MBLOCKS, PTS_SUB), ((0, 4), (1, 16)), -0.2, 0.2)), 0.1, 1.0)
    return {"hidden": hidden, "noise_seeds": noise_seeds, "noise_table": noise_table, "inner_weight": inner_weight, "inner_bias": inner_bias, "output_weight": output_weight, "output_bias": output_bias, "state_bank": state_bank, "ic_index": ic_index, "target_index": target_index, "area_weight": area_weight}


FAIR_ALPHA = 0.95

def reference(hidden, noise_seeds, noise_table, inner_weight, inner_bias, output_weight, output_bias, state_bank, ic_index, target_index, area_weight):
    sample_count, member_count, point_count, hidden_width = hidden.shape
    variables = output_weight.shape[0]
    flat_bank = state_bank.reshape(state_bank.shape[0], variables, point_count)
    point_weight = area_weight.reshape(point_count)
    noise_rows = noise_table[noise_seeds]
    member_shift = jnp.broadcast_to(noise_rows[None], (sample_count, member_count, hidden_width)).reshape(sample_count * member_count, hidden_width)
    row_blocks = hidden.reshape(sample_count * member_count, point_count, hidden_width)
    epsilon = (1.0 - FAIR_ALPHA) / member_count
    pair_scale = (1.0 - epsilon) / (member_count * (member_count - 1.0))

    def make_noisy(row_block, shift_row):
        return (row_block.astype(jnp.float32) + shift_row[None, :]).astype(jnp.bfloat16)

    def forward(item):
        row_block, shift_row = item
        noisy = make_noisy(row_block, shift_row)
        pre_act = jnp.dot(noisy, inner_weight, preferred_element_type=jnp.float32) + inner_bias
        activation = jax.nn.gelu(pre_act).astype(jnp.bfloat16)
        return lax.dot_general(output_weight, activation, (((1,), (1,)), ((), ())), preferred_element_type=jnp.float32) + output_bias[:, None]
    predictions = lax.map(forward, (row_blocks, member_shift)).reshape(sample_count, member_count, variables, point_count)

    def score_sample(item):
        prediction, ic_row, target_row = item
        ensemble = prediction + flat_bank[ic_row][None]
        truth_field = flat_bank[target_row]
        errors = ensemble - truth_field[None]
        skill_sum = lax.optimization_barrier(jnp.sum(jnp.abs(errors), axis=0))

        def pair_step(running, other):
            spread_sum, sign_sums = running
            difference = ensemble - other[None]
            return ((spread_sum + lax.optimization_barrier(jnp.sum(jnp.abs(difference), axis=0)), sign_sums + jnp.sign(difference)), None)
        start_state = (jnp.zeros(truth_field.shape, jnp.float32), jnp.zeros(ensemble.shape, jnp.float32))
        (spread_sum, sign_sums), _ = lax.scan(pair_step, start_state, ensemble)
        crps_field = skill_sum / member_count - 0.5 * pair_scale * spread_sum
        sample_total = jnp.sum(point_weight * crps_field)
        member_grad = (point_weight / sample_count * (jnp.sign(errors) / member_count - pair_scale * sign_sums)).astype(jnp.bfloat16)
        return (sample_total, member_grad)
    totals, member_grads = lax.map(score_sample, (predictions, ic_index, target_index))
    loss = jnp.sum(totals) / (sample_count * point_count * variables)
    grad_blocks = member_grads.reshape(sample_count * member_count, variables, point_count)

    def backward(running, item):
        row_block, shift_row, member_grad = item
        grad_w1, grad_b1, grad_w2, grad_b2 = running
        noisy = make_noisy(row_block, shift_row)
        pre_act = jnp.dot(noisy, inner_weight, preferred_element_type=jnp.float32) + inner_bias
        activation, gelu_back = jax.vjp(jax.nn.gelu, pre_act)
        activation = activation.astype(jnp.bfloat16)
        grad_b2 = grad_b2 + lax.optimization_barrier(jnp.sum(member_grad.astype(jnp.float32), axis=1))
        grad_w2 = grad_w2 + jnp.dot(member_grad, activation, preferred_element_type=jnp.float32)
        carried = lax.dot_general(member_grad, output_weight, (((0,), (0,)), ((), ())), preferred_element_type=jnp.float32)
        pre_grad = gelu_back(carried)[0].astype(jnp.bfloat16)
        grad_b1 = grad_b1 + lax.optimization_barrier(jnp.sum(pre_grad.astype(jnp.float32), axis=0))
        grad_w1 = grad_w1 + lax.dot_general(noisy, pre_grad, (((0,), (0,)), ((), ())), preferred_element_type=jnp.float32)
        return ((grad_w1, grad_b1, grad_w2, grad_b2), None)
    start_grads = (jnp.zeros((hidden_width, hidden_width), jnp.float32), jnp.zeros((hidden_width,), jnp.float32), jnp.zeros((variables, hidden_width), jnp.float32), jnp.zeros((variables,), jnp.float32))
    (grad_w1, grad_b1, grad_w2, grad_b2), _ = lax.scan(backward, start_grads, (row_blocks, member_shift, grad_blocks))
    return (grad_w1, grad_b1, grad_w2, grad_b2, loss)
```

```python
import jax
import jax.numpy as jnp
from jax import lax
from jax.experimental import pallas as pl
from jax.experimental.pallas import tpu as pltpu
from jax.sharding import PartitionSpec as P

FAIR_ALPHA = 0.95
MESH = pl.DeviceIdType.MESH
BLOCKS = 4


def place():
    cuts, member, x = lax.axis_index("cuts"), lax.axis_index("member"), lax.axis_index("grid")
    core, z_hi = lax.rem(cuts, 2), lax.div(cuts, 2)
    y, z_lo = lax.div(member, 4), lax.rem(member, 4)
    return core, x, y, z_hi * 4 + z_lo


def device(core, x, y, z):
    return (lax.div(z, 4) * 2 + core, y * 4 + lax.rem(z, 4), x)


def partners(spot):
    core, x, y, z = spot
    found = [device(1 - core, x, y, z)]
    found += [device(core, lax.rem(x + k, 4), y, z) for k in range(1, 4)]
    found += [device(core, x, lax.rem(y + k, 4), z) for k in range(1, 4)]
    found += [device(core, x, y, lax.rem(z + k, 8)) for k in range(1, 8)]
    return found


def greet(devices):
    barrier = pltpu.get_barrier_semaphore()
    for one in devices:
        pl.semaphore_signal(barrier, inc=1, device_id=one, device_id_type=MESH)
    pl.semaphore_wait(barrier, len(devices))


class Total:
    def __init__(self, spot, acc, out, pair, part1, got1, part2, got2, ztx, zrx, ztile, zall, sems):
        self.spot, self.acc, self.out = spot, acc, out
        self.pair, self.part1, self.got1, self.part2, self.got2 = pair, part1, got1, part2, got2
        self.ztx, self.zrx, self.ztile, self.zall = ztx, zrx, ztile, zall
        (self.pair_s, self.pair_r, self.s1, self.r1, self.s2, self.r2, self.zs, self.zr,
         self.gz_s, self.gz_r, self.g2_s, self.g2_r, self.g1_s, self.g1_r, self.gp_s, self.gp_r) = sems

    def axes(self, block):
        _, x, y, _ = self.spot
        return (x, y) if block % 2 == 0 else (y, x)

    def along(self, block, phase, k):
        core, x, y, z = self.spot
        if (block + phase) % 2 == 0:
            return device(core, lax.rem(x + k, 4), y, z)
        return device(core, x, lax.rem(y + k, 4), z)

    def columns(self, block, core):
        return pl.ds(pl.multiple_of(block * 256 + core * 128, 128), 128)

    def copy(self, src, dst, send, recv, target):
        return pltpu.make_async_remote_copy(
            src_ref=src, dst_ref=dst, send_sem=send, recv_sem=recv, device_id=target, device_id_type=MESH
        )

    def pair_copy(self, block):
        core, x, y, z = self.spot
        return self.copy(
            self.acc.at[:, self.columns(block, 1 - core)], self.pair.at[block],
            self.pair_s.at[block], self.pair_r.at[block], device(1 - core, x, y, z),
        )

    def pair_start(self, block):
        self.pair_copy(block).start()

    def pair_end(self, block):
        core = self.spot[0]
        self.pair_copy(block).wait()
        self.part1[block] = self.acc[:, self.columns(block, core)] + self.pair[block]

    def first_copy(self, block, k):
        mine = self.axes(block)[0]
        rows = pl.ds(pl.multiple_of(lax.rem(mine + k, 4) * 288, 8), 288)
        return self.copy(
            self.part1.at[block, rows], self.got1.at[block, k - 1],
            self.s1.at[block, k - 1], self.r1.at[block, k - 1], self.along(block, 0, k),
        )

    def first_start(self, block):
        for k in range(1, 4):
            self.first_copy(block, k).start()

    def first_end(self, block):
        mine = self.axes(block)[0]
        for k in range(1, 4):
            self.first_copy(block, k).wait()
        own = self.part1[block, pl.ds(pl.multiple_of(mine * 288, 8), 288)]
        self.part2[block] = (own + self.got1[block, 0]) + (self.got1[block, 1] + self.got1[block, 2])

    def second_copy(self, block, k):
        mine = self.axes(block)[1]
        rows = pl.ds(pl.multiple_of(lax.rem(mine + k, 4) * 72, 8), 72)
        return self.copy(
            self.part2.at[block, rows], self.got2.at[block, k - 1],
            self.s2.at[block, k - 1], self.r2.at[block, k - 1], self.along(block, 1, k),
        )

    def second_start(self, block):
        for k in range(1, 4):
            self.second_copy(block, k).start()

    def second_end(self, block):
        mine = self.axes(block)[1]
        for k in range(1, 4):
            self.second_copy(block, k).wait()
        own = self.part2[block, pl.ds(pl.multiple_of(mine * 72, 8), 72)]
        total = (own + self.got2[block, 0]) + (self.got2[block, 1] + self.got2[block, 2])
        for other in range(8):
            self.ztx[other, block, 0:8] = total[8 * other : 8 * other + 8]
            self.ztx[other, block, 8:16] = total[64:72]

    def z_copy(self, k):
        core, x, y, z = self.spot
        other = lax.rem(z + k, 8)
        return self.copy(
            self.ztx.at[other], self.zrx.at[z], self.zs.at[k - 1], self.zr.at[k - 1], device(core, x, y, other)
        )

    def z_start(self):
        z = self.spot[3]
        for k in range(1, 8):
            self.z_copy(k).start()
        self.zrx[z] = self.ztx[z]

    def z_end(self):
        core, x, y, z = self.spot
        for k in range(1, 8):
            self.z_copy(k).wait_send()
            origin = lax.rem(z + 8 - k, 8)
            self.copy(
                self.ztx.at[z], self.zrx.at[origin], self.zs.at[k - 1], self.zr.at[k - 1], device(core, x, y, origin)
            ).wait_recv()
        total = self.zrx[0]
        for other in range(1, 8):
            total = total + self.zrx[other]
        self.ztile[...] = total

    def gather_z_copy(self, k, spot_z):
        core, x, y, z = self.spot
        return self.copy(
            self.ztile.at[:, 0:8], self.zall.at[spot_z], self.gz_s.at[k - 1], self.gz_r.at[k - 1],
            device(core, x, y, lax.rem(z + k, 8)),
        )

    def gather_z_start(self):
        z = self.spot[3]
        for k in range(1, 8):
            self.gather_z_copy(k, z).start()
        self.zall[z] = self.ztile[:, 0:8]

    def chunk(self, block):
        one, two = self.axes(block)
        return one * 288 + two * 72

    def gather_z_end(self):
        core, _, _, z = self.spot
        for k in range(1, 8):
            self.gather_z_copy(k, z).wait_send()
            self.gather_z_copy(k, lax.rem(z + 8 - k, 8)).wait_recv()
        for block in range(BLOCKS):
            base = self.chunk(block)
            columns = self.columns(block, core)
            for other in range(8):
                self.out[pl.ds(pl.multiple_of(base + 8 * other, 8), 8), columns] = self.zall[other, block]
            self.out[pl.ds(pl.multiple_of(base + 64, 8), 8), columns] = self.ztile[block, 8:16]

    def gather_copy(self, block, phase, k, sender):
        core = self.spot[0]
        one, two = self.axes(block)
        if phase == 1:
            if sender:
                two = lax.rem(two + 4 - k, 4)
            rows, size, send, recv = one * 288 + two * 72, 72, self.g2_s, self.g2_r
        else:
            if sender:
                one = lax.rem(one + 4 - k, 4)
            rows, size, send, recv = one * 288, 288, self.g1_s, self.g1_r
        spot = self.out.at[pl.ds(pl.multiple_of(rows, 8), size), self.columns(block, core)]
        return self.copy(spot, spot, send.at[block, k - 1], recv.at[block, k - 1], self.along(block, phase, k))

    def gather_start(self, block, phase):
        for k in range(1, 4):
            self.gather_copy(block, phase, k, False).start()

    def gather_end(self, block, phase):
        for k in range(1, 4):
            self.gather_copy(block, phase, k, False).wait_send()
            self.gather_copy(block, phase, k, True).wait_recv()

    def gather_pair_copy(self, block, core_of):
        core, x, y, z = self.spot
        spot = self.out.at[:, self.columns(block, core_of)]
        return self.copy(spot, spot, self.gp_s.at[block], self.gp_r.at[block], device(1 - core, x, y, z))

    def gather_pair_start(self, block):
        self.gather_pair_copy(block, self.spot[0]).start()

    def gather_pair_end(self, block):
        self.gather_pair_copy(block, self.spot[0]).wait_send()
        self.gather_pair_copy(block, 1 - self.spot[0]).wait_recv()

    def finish(self):
        blocks = range(BLOCKS)
        self.z_start()
        self.z_end()
        self.gather_z_start()
        self.gather_z_end()
        for b in blocks:
            self.gather_start(b, 1)
        for b in blocks:
            self.gather_end(b, 1)
            self.gather_start(b, 0)
        for b in blocks:
            self.gather_end(b, 0)
            self.gather_pair_start(b)
        for b in blocks:
            self.gather_pair_end(b)


def total_scratch():
    f32 = jnp.float32
    dma = pltpu.SemaphoreType.DMA
    buffers = [
        pltpu.VMEM((BLOCKS, 1152, 128), f32),
        pltpu.VMEM((BLOCKS, 1152, 128), f32),
        pltpu.VMEM((BLOCKS, 3, 288, 128), f32),
        pltpu.VMEM((BLOCKS, 288, 128), f32),
        pltpu.VMEM((BLOCKS, 3, 72, 128), f32),
        pltpu.VMEM((8, BLOCKS, 16, 128), f32),
        pltpu.VMEM((8, BLOCKS, 16, 128), f32),
        pltpu.VMEM((BLOCKS, 16, 128), f32),
        pltpu.VMEM((8, BLOCKS, 8, 128), f32),
    ]
    shapes = [(BLOCKS,), (BLOCKS, 3), (BLOCKS, 3), (7,), (7,), (BLOCKS, 3), (BLOCKS, 3), (BLOCKS,)]
    sems = []
    for shape in shapes:
        sems += [dma(shape), dma(shape)]
    return buffers, sems


def total_kernel(acc, out, *scratch):
    spot = place()
    greet(partners(spot))
    job = Total(spot, acc, out, *scratch[:9], scratch[9:])
    blocks = range(BLOCKS)
    for b in blocks:
        job.pair_start(b)
    for b in blocks:
        job.pair_end(b)
        job.first_start(b)
    for b in blocks:
        job.first_end(b)
        job.second_start(b)
    for b in blocks:
        job.second_end(b)
    job.finish()


def all_total(acc):
    buffers, sems = total_scratch()
    return pl.pallas_call(
        total_kernel,
        out_shape=jax.ShapeDtypeStruct(acc.shape, jnp.float32),
        in_specs=[pl.BlockSpec(memory_space=pltpu.VMEM)],
        out_specs=pl.BlockSpec(memory_space=pltpu.VMEM),
        scratch_shapes=buffers + sems,
        compiler_params=pltpu.CompilerParams(
            collective_id=0, has_side_effects=True, vmem_limit_bytes=48 * 1024 * 1024
        ),
    )(acc)


def body(
    hidden,
    noise_seeds,
    noise_table,
    inner_weight,
    inner_bias,
    output_weight,
    output_bias,
    state_bank,
    ic_index,
    target_index,
    area_weight,
):
    members_here = hidden.shape[1]
    points_here = hidden.shape[2]
    hidden_width = hidden.shape[3]
    variables = output_weight.shape[0]
    seed_ids = jnp.arange(noise_table.shape[0], dtype=jnp.int32)
    seeds_onehot = (noise_seeds[:, None] == seed_ids[None, :]).astype(jnp.float32)
    noise_rows = jnp.dot(
        seeds_onehot,
        noise_table,
        precision=lax.Precision.HIGHEST,
        preferred_element_type=jnp.float32,
    )
    noisy = (hidden[0].astype(jnp.float32) + noise_rows[:, None, :]).astype(jnp.bfloat16)
    noisy = noisy.reshape(members_here * points_here, hidden_width)
    pre_act = jnp.dot(noisy, inner_weight, preferred_element_type=jnp.float32) + inner_bias
    activation, gelu_back = jax.vjp(jax.nn.gelu, pre_act)
    activation = activation.astype(jnp.bfloat16)
    prediction = (
        lax.dot_general(
            output_weight, activation, (((1,), (1,)), ((), ())), preferred_element_type=jnp.float32
        )
        + output_bias[:, None]
    )
    prediction = prediction.reshape(variables, members_here, points_here)
    point_pred = lax.all_to_all(prediction, "member", split_axis=2, concat_axis=1, tiled=True)
    member_count = point_pred.shape[1]
    flat_bank = state_bank[:, :, 0, 0, :]
    ic_state = lax.dynamic_index_in_dim(flat_bank, ic_index[0], 0, keepdims=False)
    truth_field = lax.dynamic_index_in_dim(flat_bank, target_index[0], 0, keepdims=False)
    ensemble = point_pred + ic_state[:, None, :]
    point_weight = area_weight[0, 0]
    sample_count = lax.axis_size("cuts") * hidden.shape[0]
    total_points = lax.axis_size("grid") * points_here
    epsilon = (1.0 - FAIR_ALPHA) / member_count
    pair_scale = (1.0 - epsilon) / (member_count * (member_count - 1.0))
    errors = ensemble - truth_field[:, None, :]
    differences = ensemble[:, :, None, :] - ensemble[:, None, :, :]
    skill_sum = jnp.sum(jnp.abs(errors), axis=1)
    spread_sum = jnp.sum(jnp.abs(differences), axis=(1, 2))
    sign_sums = jnp.sum(jnp.sign(differences), axis=2)
    crps_field = skill_sum / member_count - 0.5 * pair_scale * spread_sum
    local_loss = jnp.sum(point_weight * crps_field) / (sample_count * total_points * variables)
    member_grad = (
        point_weight / sample_count * (jnp.sign(errors) / member_count - pair_scale * sign_sums)
    ).astype(jnp.bfloat16)
    returned = lax.all_to_all(member_grad, "member", split_axis=1, concat_axis=2, tiled=True)
    returned = returned.reshape(variables, members_here * points_here)
    grad_b2 = jnp.sum(returned.astype(jnp.float32), axis=1)
    grad_w2 = jnp.dot(returned, activation, preferred_element_type=jnp.float32)
    carried = lax.dot_general(
        returned, output_weight, (((0,), (0,)), ((), ())), preferred_element_type=jnp.float32
    )
    pre_grad = gelu_back(carried)[0].astype(jnp.bfloat16)
    grad_b1 = jnp.sum(pre_grad.astype(jnp.float32), axis=0)
    grad_w1 = lax.dot_general(
        noisy, pre_grad, (((0,), (0,)), ((), ())), preferred_element_type=jnp.float32
    )
    rows = jnp.zeros((28, hidden_width), jnp.float32)
    rows = rows.at[0].set(grad_b1).at[1, :variables].set(grad_b2).at[1, variables].set(local_loss)
    second = jnp.concatenate([grad_w2, rows], axis=0)
    packed = jnp.concatenate([grad_w1.reshape(4, 4, 64, hidden_width), second.reshape(4, 4, 8, hidden_width)], axis=2)
    summed = all_total(packed.reshape(1152, hidden_width)).reshape(4, 4, 72, hidden_width)
    grad_w1 = summed[:, :, :64].reshape(hidden_width, hidden_width)
    second = summed[:, :, 64:].reshape(128, hidden_width)
    return (
        grad_w1,
        second[variables],
        second[:variables],
        second[variables + 1, :variables],
        second[variables + 1, variables],
    )


def solution(mesh):
    return jax.shard_map(
        body,
        mesh=mesh,
        in_specs=(
            P("cuts", "member", "grid", None),
            P("member"),
            P(),
            P(),
            P(),
            P(),
            P(),
            P(None, None, "grid", "member", None),
            P("cuts"),
            P("cuts"),
            P("grid", "member", None),
        ),
        out_specs=(P(), P(), P(), P(), P()),
        check_vma=False,
    )
```

```python
import jax
import jax.numpy as jnp
from jax import lax
from jax.experimental import pallas as pl
from jax.experimental.pallas import tpu as pltpu
from jax.sharding import PartitionSpec as P

FAIR_ALPHA = 0.95
MESH = pl.DeviceIdType.MESH
BLOCKS = 4


def place():
    cuts, member, x = lax.axis_index("cuts"), lax.axis_index("member"), lax.axis_index("grid")
    core, z_hi = lax.rem(cuts, 2), lax.div(cuts, 2)
    y, z_lo = lax.div(member, 4), lax.rem(member, 4)
    return core, x, y, z_hi * 4 + z_lo


def device(core, x, y, z):
    return (lax.div(z, 4) * 2 + core, y * 4 + lax.rem(z, 4), x)


def partners(spot):
    core, x, y, z = spot
    found = [device(1 - core, x, y, z)]
    found += [device(core, lax.rem(x + k, 4), y, z) for k in range(1, 4)]
    found += [device(core, x, lax.rem(y + k, 4), z) for k in range(1, 4)]
    found += [device(core, x, y, lax.rem(z + k, 8)) for k in range(1, 8)]
    return found


def greet(devices):
    barrier = pltpu.get_barrier_semaphore()
    for one in devices:
        pl.semaphore_signal(barrier, inc=1, device_id=one, device_id_type=MESH)
    pl.semaphore_wait(barrier, len(devices))


class Total:
    def __init__(self, spot, acc, out, pair, part1, got1, part2, got2, ztx, zrx, ztile, zall, sems):
        self.spot, self.acc, self.out = spot, acc, out
        self.pair, self.part1, self.got1, self.part2, self.got2 = pair, part1, got1, part2, got2
        self.ztx, self.zrx, self.ztile, self.zall = ztx, zrx, ztile, zall
        (self.pair_s, self.pair_r, self.s1, self.r1, self.s2, self.r2, self.zs, self.zr,
         self.gz_s, self.gz_r, self.g2_s, self.g2_r, self.g1_s, self.g1_r, self.gp_s, self.gp_r) = sems

    def axes(self, block):
        _, x, y, _ = self.spot
        return (x, y) if block % 2 == 0 else (y, x)

    def along(self, block, phase, k):
        core, x, y, z = self.spot
        if (block + phase) % 2 == 0:
            return device(core, lax.rem(x + k, 4), y, z)
        return device(core, x, lax.rem(y + k, 4), z)

    def columns(self, block, core):
        return pl.ds(pl.multiple_of(block * 256 + core * 128, 128), 128)

    def copy(self, src, dst, send, recv, target):
        return pltpu.make_async_remote_copy(
            src_ref=src, dst_ref=dst, send_sem=send, recv_sem=recv, device_id=target, device_id_type=MESH
        )

    def pair_copy(self, block):
        core, x, y, z = self.spot
        return self.copy(
            self.acc.at[:, self.columns(block, 1 - core)], self.pair.at[block],
            self.pair_s.at[block], self.pair_r.at[block], device(1 - core, x, y, z),
        )

    def pair_start(self, block):
        self.pair_copy(block).start()

    def pair_end(self, block):
        core = self.spot[0]
        self.pair_copy(block).wait()
        self.part1[block] = self.acc[:, self.columns(block, core)] + self.pair[block]

    def first_copy(self, block, k):
        mine = self.axes(block)[0]
        rows = pl.ds(pl.multiple_of(lax.rem(mine + k, 4) * 288, 8), 288)
        return self.copy(
            self.part1.at[block, rows], self.got1.at[block, k - 1],
            self.s1.at[block, k - 1], self.r1.at[block, k - 1], self.along(block, 0, k),
        )

    def first_start(self, block):
        for k in range(1, 4):
            self.first_copy(block, k).start()

    def first_end(self, block):
        mine = self.axes(block)[0]
        for k in range(1, 4):
            self.first_copy(block, k).wait()
        own = self.part1[block, pl.ds(pl.multiple_of(mine * 288, 8), 288)]
        self.part2[block] = (own + self.got1[block, 0]) + (self.got1[block, 1] + self.got1[block, 2])

    def second_copy(self, block, k):
        mine = self.axes(block)[1]
        rows = pl.ds(pl.multiple_of(lax.rem(mine + k, 4) * 72, 8), 72)
        return self.copy(
            self.part2.at[block, rows], self.got2.at[block, k - 1],
            self.s2.at[block, k - 1], self.r2.at[block, k - 1], self.along(block, 1, k),
        )

    def second_start(self, block):
        for k in range(1, 4):
            self.second_copy(block, k).start()

    def second_end(self, block):
        mine = self.axes(block)[1]
        for k in range(1, 4):
            self.second_copy(block, k).wait()
        own = self.part2[block, pl.ds(pl.multiple_of(mine * 72, 8), 72)]
        total = (own + self.got2[block, 0]) + (self.got2[block, 1] + self.got2[block, 2])
        for other in range(8):
            self.ztx[other, block, 0:8] = total[8 * other : 8 * other + 8]
            self.ztx[other, block, 8:16] = total[64:72]

    def z_copy(self, k):
        core, x, y, z = self.spot
        other = lax.rem(z + k, 8)
        return self.copy(
            self.ztx.at[other], self.zrx.at[z], self.zs.at[k - 1], self.zr.at[k - 1], device(core, x, y, other)
        )

    def z_start(self):
        z = self.spot[3]
        for k in range(1, 8):
            self.z_copy(k).start()
        self.zrx[z] = self.ztx[z]

    def z_end(self):
        core, x, y, z = self.spot
        for k in range(1, 8):
            self.z_copy(k).wait_send()
            origin = lax.rem(z + 8 - k, 8)
            self.copy(
                self.ztx.at[z], self.zrx.at[origin], self.zs.at[k - 1], self.zr.at[k - 1], device(core, x, y, origin)
            ).wait_recv()
        total = self.zrx[0]
        for other in range(1, 8):
            total = total + self.zrx[other]
        self.ztile[...] = total

    def gather_z_copy(self, k, spot_z):
        core, x, y, z = self.spot
        return self.copy(
            self.ztile.at[:, 0:8], self.zall.at[spot_z], self.gz_s.at[k - 1], self.gz_r.at[k - 1],
            device(core, x, y, lax.rem(z + k, 8)),
        )

    def gather_z_start(self):
        z = self.spot[3]
        for k in range(1, 8):
            self.gather_z_copy(k, z).start()
        self.zall[z] = self.ztile[:, 0:8]

    def chunk(self, block):
        one, two = self.axes(block)
        return one * 288 + two * 72

    def gather_z_end(self):
        core, _, _, z = self.spot
        for k in range(1, 8):
            self.gather_z_copy(k, z).wait_send()
            self.gather_z_copy(k, lax.rem(z + 8 - k, 8)).wait_recv()
        for block in range(BLOCKS):
            base = self.chunk(block)
            columns = self.columns(block, core)
            for other in range(8):
                self.out[pl.ds(pl.multiple_of(base + 8 * other, 8), 8), columns] = self.zall[other, block]
            self.out[pl.ds(pl.multiple_of(base + 64, 8), 8), columns] = self.ztile[block, 8:16]

    def gather_copy(self, block, phase, k, sender):
        core = self.spot[0]
        one, two = self.axes(block)
        if phase == 1:
            if sender:
                two = lax.rem(two + 4 - k, 4)
            rows, size, send, recv = one * 288 + two * 72, 72, self.g2_s, self.g2_r
        else:
            if sender:
                one = lax.rem(one + 4 - k, 4)
            rows, size, send, recv = one * 288, 288, self.g1_s, self.g1_r
        spot = self.out.at[pl.ds(pl.multiple_of(rows, 8), size), self.columns(block, core)]
        return self.copy(spot, spot, send.at[block, k - 1], recv.at[block, k - 1], self.along(block, phase, k))

    def gather_start(self, block, phase):
        for k in range(1, 4):
            self.gather_copy(block, phase, k, False).start()

    def gather_end(self, block, phase):
        for k in range(1, 4):
            self.gather_copy(block, phase, k, False).wait_send()
            self.gather_copy(block, phase, k, True).wait_recv()

    def gather_pair_copy(self, block, core_of):
        core, x, y, z = self.spot
        spot = self.out.at[:, self.columns(block, core_of)]
        return self.copy(spot, spot, self.gp_s.at[block], self.gp_r.at[block], device(1 - core, x, y, z))

    def gather_pair_start(self, block):
        self.gather_pair_copy(block, self.spot[0]).start()

    def gather_pair_end(self, block):
        self.gather_pair_copy(block, self.spot[0]).wait_send()
        self.gather_pair_copy(block, 1 - self.spot[0]).wait_recv()

    def finish(self):
        blocks = range(BLOCKS)
        self.z_start()
        self.z_end()
        self.gather_z_start()
        self.gather_z_end()
        for b in blocks:
            self.gather_start(b, 1)
        for b in blocks:
            self.gather_end(b, 1)
            self.gather_start(b, 0)
        for b in blocks:
            self.gather_end(b, 0)
            self.gather_pair_start(b)
        for b in blocks:
            self.gather_pair_end(b)


def total_scratch():
    f32 = jnp.float32
    dma = pltpu.SemaphoreType.DMA
    buffers = [
        pltpu.VMEM((BLOCKS, 1152, 128), f32),
        pltpu.VMEM((BLOCKS, 1152, 128), f32),
        pltpu.VMEM((BLOCKS, 3, 288, 128), f32),
        pltpu.VMEM((BLOCKS, 288, 128), f32),
        pltpu.VMEM((BLOCKS, 3, 72, 128), f32),
        pltpu.VMEM((8, BLOCKS, 16, 128), f32),
        pltpu.VMEM((8, BLOCKS, 16, 128), f32),
        pltpu.VMEM((BLOCKS, 16, 128), f32),
        pltpu.VMEM((8, BLOCKS, 8, 128), f32),
    ]
    shapes = [(BLOCKS,), (BLOCKS, 3), (BLOCKS, 3), (7,), (7,), (BLOCKS, 3), (BLOCKS, 3), (BLOCKS,)]
    sems = []
    for shape in shapes:
        sems += [dma(shape), dma(shape)]
    return buffers, sems


VARS_PAD = 112
ROOT = 0.7978845608028654
CUBE = 0.044715


def chunk_rows(start, size):
    return pl.ds(pl.multiple_of(start, 128), size)


def step_kernel(
    seed, ic, target, hidden, table, w1, b1, w2, b2, bank, weight, out,
    noisy, noisy_t, pre, act, pred, ens, grad_send, grad_t, part_grad, acc, *rest
):
    buffers, sems = rest[:9], rest[9:25]
    pred_s, pred_r, ret_s, ret_r = rest[25:]
    spot = place()
    core, x, y, z = spot
    z_hi, z_lo = lax.div(z, 4), lax.rem(z, 4)
    me = y * 4 + z_lo
    others = [(t, i) for t in range(4) for i in range(4) if t + i > 0]

    def member_at(t, i):
        return lax.rem(y + t, 4) * 4 + lax.rem(z_lo + i, 4)

    def member_device(member):
        return (lax.axis_index("cuts"), member, x)

    known = [member_device(member_at(t, i)) for t, i in others]
    known += [device(1 - core, x, y, z)]
    known += [device(core, lax.rem(x + k, 4), y, z) for k in range(1, 4)]
    known += [device(core, x, y, (1 - z_hi) * 4 + k) for k in range(4)]
    greet(known)

    def pred_copy(t, i, source):
        owner = member_at(t, i)
        slot = 4 * t + i - 1
        return pltpu.make_async_remote_copy(
            src_ref=pred.at[owner, 0:104], dst_ref=ens.at[source, 0:104],
            send_sem=pred_s.at[slot], recv_sem=pred_r.at[slot],
            device_id=member_device(owner), device_id_type=MESH,
        )

    def back_copy(t, i, source):
        owner = member_at(t, i)
        slot = 4 * t + i - 1
        return pltpu.make_async_remote_copy(
            src_ref=grad_send.at[owner], dst_ref=grad_t.at[:, chunk_rows(source * 128, 128)],
            send_sem=ret_s.at[slot], recv_sem=ret_r.at[slot],
            device_id=member_device(owner), device_id_type=MESH,
        )

    def source_of(t, i):
        return lax.rem(y + 4 - t, 4) * 4 + lax.rem(z_lo + 4 - i, 4)

    noise = table[pl.ds(seed[0], 1), :]

    for t in range(4):
        top = lax.rem(y + t, 4) * 512

        def add_noise(q, _):
            rows = chunk_rows(top + q * 128, 128)
            noisy[rows, :] = (hidden[rows, :].astype(jnp.float32) + noise).astype(jnp.bfloat16)
            return 0

        lax.fori_loop(0, 4, add_noise, 0)
        rows = chunk_rows(top, 512)

        def inner(n, _):
            columns = chunk_rows(n * 256, 256)
            v = jnp.dot(noisy[rows, :], w1[:, columns], preferred_element_type=jnp.float32) + b1[:, columns]
            pre[rows, columns] = v
            bend = jnp.tanh(v * (ROOT + (ROOT * CUBE) * (v * v)))
            half = 0.5 * v
            act[rows, columns] = (half + half * bend).astype(jnp.bfloat16)
            return 0

        lax.fori_loop(0, 4, inner, 0)
        guess = lax.dot_general(
            w2[...], act[rows, :], (((1,), (1,)), ((), ())), preferred_element_type=jnp.float32
        ) + b2[...]
        base = lax.rem(y + t, 4) * 4
        for i in range(4):
            pred[base + i] = guess[:, 128 * i : 128 * i + 128]
        for i in range(4):
            if t + i > 0:
                pred_copy(t, i, me).start()
    ens[me] = pred[me]

    def bend_back(r, _):
        rows = chunk_rows(r * 128, 128)

        def piece(n, _):
            columns = chunk_rows(n * 256, 256)
            v = pre[rows, columns]
            square = v * v
            bend = jnp.tanh(v * (ROOT + (ROOT * CUBE) * square))
            slope = ROOT + (3.0 * ROOT * CUBE) * square
            pre[rows, columns] = 0.5 * ((1.0 + bend) + (v * slope) * (1.0 - bend * bend))
            return 0

        lax.fori_loop(0, 4, piece, 0)
        return 0

    lax.fori_loop(0, 16, bend_back, 0)

    def turn(r, _):
        rows = chunk_rows(r * 256, 256)

        def piece(n, _):
            columns = chunk_rows(n * 256, 256)
            noisy_t[columns, rows] = noisy[rows, columns].T
            return 0

        lax.fori_loop(0, 4, piece, 0)
        return 0

    lax.fori_loop(0, 8, turn, 0)

    for t, i in others:
        pred_copy(t, i, me).wait_send()
        pred_copy(t, i, source_of(t, i)).wait_recv()

    epsilon = (1.0 - FAIR_ALPHA) / 16
    pair_scale = (1.0 - epsilon) / (16 * 15.0)
    area = weight[...]

    def score(start, size):
        rows = pl.ds(start, size)
        first = bank[ic[0], rows, :]
        truth = bank[target[0], rows, :]
        values = [ens[m, rows, :] + first for m in range(16)]
        ranks = [None] * 16
        for a in range(16):
            for b in range(a + 1, 16):
                low = values[a] < values[b]
                high = values[a] > values[b]
                sign = jnp.where(high, 1.0, jnp.where(low, -1.0, 0.0))
                ranks[a] = sign if ranks[a] is None else ranks[a] + sign
                ranks[b] = -sign if ranks[b] is None else ranks[b] - sign
        skill = jnp.zeros((size, 128), jnp.float32)
        spread = jnp.zeros((size, 128), jnp.float32)
        for m in range(16):
            error = values[m] - truth
            skill = skill + jnp.abs(error)
            spread = spread + error * ranks[m]
            side = jnp.where(values[m] > truth, 1.0, jnp.where(values[m] < truth, -1.0, 0.0))
            ens[m, rows, :] = (area / 4) * (side / 16 - pair_scale * ranks[m])
        return area * (skill / 16 - pair_scale * spread)

    def score_step(s, total):
        return total + score(pl.multiple_of(s * 8, 8), 8)

    total = lax.fori_loop(0, 12, score_step, jnp.zeros((8, 128), jnp.float32))
    total = jnp.sum(total, axis=0, keepdims=True) + jnp.sum(score(96, 4), axis=0, keepdims=True)
    total = total / (4.0 * 8192 * 100)

    inside = lax.broadcasted_iota(jnp.int32, (VARS_PAD, 128), 0) < 100
    for t, i in [(0, 0)] + others:
        owner = member_at(t, i)
        value = jnp.where(inside, ens[owner], 0.0).astype(jnp.bfloat16)
        if t + i > 0:
            grad_send[owner] = value
            back_copy(t, i, me).start()
        else:
            grad_t[:, chunk_rows(me * 128, 128)] = value
    for t, i in others:
        back_copy(t, i, me).wait_send()
        back_copy(t, i, source_of(t, i)).wait_recv()

    job = Total(spot, acc, out, *buffers, sems)
    ones = jnp.ones((16, 2048), jnp.bfloat16)
    bias_row = lax.dot_general(
        ones, grad_t[...], (((1,), (1,)), ((), ())), preferred_element_type=jnp.float32
    )[0:1]
    bias_row = jnp.concatenate([bias_row, jnp.zeros((1, 16), jnp.float32)], axis=1)

    def packed_row(r):
        return (r // 32) * 288 + (r % 32) // 8 * 72 + 64

    def backward(block):
        columns = pl.ds(block * 256, 256)

        def spread_back(r, bias):
            rows = chunk_rows(r * 512, 512)
            carried = lax.dot_general(
                grad_t[:, rows], w2[:, columns], (((0,), (0,)), ((), ())), preferred_element_type=jnp.float32
            )
            value = (carried * pre[rows, columns]).astype(jnp.bfloat16)
            part_grad[rows, :] = value
            return bias + jnp.sum(value.astype(jnp.float32), axis=0, keepdims=True)

        bias = lax.fori_loop(0, 4, spread_back, jnp.zeros((1, 256), jnp.float32))

        def weights(q, _):
            wide = jnp.dot(noisy_t[chunk_rows(q * 256, 256), :], part_grad[...], preferred_element_type=jnp.float32)
            for c in range(4):
                acc[pl.ds(pl.multiple_of(q * 288 + 72 * c, 8), 64), columns] = wide[64 * c : 64 * c + 64]
            return 0

        lax.fori_loop(0, 4, weights, 0)
        second = jnp.dot(grad_t[...], act[:, columns], preferred_element_type=jnp.float32)
        for r in range(0, VARS_PAD, 8):
            acc[pl.ds(packed_row(r), 8), columns] = second[r : r + 8]
        row = packed_row(112)
        acc[pl.ds(row, 8), columns] = jnp.zeros((8, 256), jnp.float32)
        acc[pl.ds(packed_row(120), 8), columns] = jnp.zeros((8, 256), jnp.float32)
        acc[pl.ds(row, 1), columns] = bias
        if block == 0:
            acc[pl.ds(row + 1, 1), pl.ds(0, 128)] = bias_row
            acc[pl.ds(row + 1, 1), pl.ds(128, 128)] = total

    for block in range(BLOCKS):
        backward(block)
        job.pair_start(block)
        if block >= 1:
            job.pair_end(block - 1)
            job.first_start(block - 1)
        if block >= 2:
            job.first_end(block - 2)
            job.second_start(block - 2)
        if block >= 3:
            job.second_end(block - 3)
    job.pair_end(3)
    job.first_start(3)
    job.first_end(2)
    job.second_start(2)
    job.first_end(3)
    job.second_start(3)
    job.second_end(1)
    job.second_end(2)
    job.second_end(3)
    job.finish()


def whole_step(seed, ic, target, *arrays):
    total_buffers, total_sems = total_scratch()
    bf16, f32 = jnp.bfloat16, jnp.float32
    dma = pltpu.SemaphoreType.DMA
    vmem = pl.BlockSpec(memory_space=pltpu.VMEM)
    smem = pl.BlockSpec(memory_space=pltpu.SMEM)
    return pl.pallas_call(
        step_kernel,
        out_shape=jax.ShapeDtypeStruct((1152, 1024), f32),
        in_specs=[smem] * 3 + [vmem] * 8,
        out_specs=vmem,
        scratch_shapes=[
            pltpu.VMEM((2048, 1024), bf16),
            pltpu.VMEM((1024, 2048), bf16),
            pltpu.VMEM((2048, 1024), f32),
            pltpu.VMEM((2048, 1024), bf16),
            pltpu.VMEM((16, VARS_PAD, 128), f32),
            pltpu.VMEM((16, VARS_PAD, 128), f32),
            pltpu.VMEM((16, VARS_PAD, 128), bf16),
            pltpu.VMEM((VARS_PAD, 2048), bf16),
            pltpu.VMEM((2048, 256), bf16),
            pltpu.VMEM((1152, 1024), f32),
        ] + total_buffers + total_sems + [dma((15,)), dma((15,)), dma((15,)), dma((15,))],
        compiler_params=pltpu.CompilerParams(
            collective_id=0, has_side_effects=True, vmem_limit_bytes=60 * 1024 * 1024
        ),
    )(seed, ic, target, *arrays)


def body(
    hidden,
    noise_seeds,
    noise_table,
    inner_weight,
    inner_bias,
    output_weight,
    output_bias,
    state_bank,
    ic_index,
    target_index,
    area_weight,
):
    variables = output_weight.shape[0]
    pad = VARS_PAD - variables
    summed = whole_step(
        noise_seeds, ic_index, target_index,
        hidden.reshape(2048, 1024),
        noise_table,
        inner_weight,
        inner_bias.reshape(1, 1024),
        jnp.pad(output_weight, ((0, pad), (0, 0))),
        jnp.pad(output_bias, (0, pad)).reshape(VARS_PAD, 1),
        state_bank.reshape(8, variables, 128),
        area_weight.reshape(1, 128),
    ).reshape(4, 4, 72, 1024)
    grad_w1 = summed[:, :, :64].reshape(1024, 1024)
    second = summed[:, :, 64:].reshape(128, 1024)
    return (
        grad_w1,
        second[112],
        second[:variables],
        second[113, :variables],
        jnp.sum(second[113, 128:256]),
    )


def solution(mesh):
    return jax.shard_map(
        body,
        mesh=mesh,
        in_specs=(
            P("cuts", "member", "grid", None),
            P("member"),
            P(),
            P(),
            P(),
            P(),
            P(),
            P(None, None, "grid", "member", None),
            P("cuts"),
            P("cuts"),
            P("grid", "member", None),
        ),
        out_specs=(P(), P(), P(), P(), P()),
        check_vma=False,
    )
```

```python
import jax
import jax.numpy as jnp
from jax import lax
from jax.experimental import pallas as pl
from jax.experimental.pallas import tpu as pltpu
from jax.sharding import PartitionSpec as P

FAIR_ALPHA = 0.95
MESH = pl.DeviceIdType.MESH
BLOCKS = 4


def place():
    cuts, member, x = lax.axis_index("cuts"), lax.axis_index("member"), lax.axis_index("grid")
    core, z_hi = lax.rem(cuts, 2), lax.div(cuts, 2)
    y, z_lo = lax.div(member, 4), lax.rem(member, 4)
    return core, x, y, z_hi * 4 + z_lo


def device(core, x, y, z):
    return (lax.div(z, 4) * 2 + core, y * 4 + lax.rem(z, 4), x)


def greet(devices):
    barrier = pltpu.get_barrier_semaphore()
    for one in devices:
        pl.semaphore_signal(barrier, inc=1, device_id=one, device_id_type=MESH)
    pl.semaphore_wait(barrier, len(devices))


WIRE = jnp.bfloat16


class Total:
    def __init__(self, spot, acc, out, pair, send1, got1, part2, got2, ztx, zrx, gtx, zall, sems):
        self.spot, self.acc, self.out = spot, acc, out
        self.pair, self.send1, self.got1, self.part2, self.got2 = pair, send1, got1, part2, got2
        self.ztx, self.zrx, self.gtx, self.zall = ztx, zrx, gtx, zall
        (self.pair_s, self.pair_r, self.s1, self.r1, self.s2, self.r2, self.zs, self.zr,
         self.gz_s, self.gz_r, self.g2_s, self.g2_r, self.g1_s, self.g1_r, self.gp_s, self.gp_r) = sems

    def axes(self, block):
        _, x, y, _ = self.spot
        return (x, y) if block % 2 == 0 else (y, x)

    def along(self, block, phase, k):
        core, x, y, z = self.spot
        if (block + phase) % 2 == 0:
            return device(core, lax.rem(x + k, 4), y, z)
        return device(core, x, lax.rem(y + k, 4), z)

    def columns(self, block, core):
        return pl.ds(pl.multiple_of(block * 256 + core * 128, 128), 128)

    def copy(self, src, dst, send, recv, target):
        return pltpu.make_async_remote_copy(
            src_ref=src, dst_ref=dst, send_sem=send, recv_sem=recv, device_id=target, device_id_type=MESH
        )

    def pair_copy(self, block):
        core, x, y, z = self.spot
        return self.copy(
            self.acc.at[:, self.columns(block, 1 - core)], self.pair.at[block],
            self.pair_s.at[block], self.pair_r.at[block], device(1 - core, x, y, z),
        )

    def pair_start(self, block):
        self.pair_copy(block).start()

    def pair_end(self, block):
        columns = self.columns(block, self.spot[0])
        self.pair_copy(block).wait()

        def add(q, _):
            rows = pl.ds(pl.multiple_of(q * 288, 32), 288)
            value = self.acc[rows, columns] + self.pair[block, rows]
            self.pair[block, rows] = value
            self.send1[block, rows] = value.astype(WIRE)
            return 0

        lax.fori_loop(0, 4, add, 0)

    def first_copy(self, block, k):
        mine = self.axes(block)[0]
        rows = pl.ds(pl.multiple_of(lax.rem(mine + k, 4) * 288, 32), 288)
        return self.copy(
            self.send1.at[block, rows], self.got1.at[block, k - 1],
            self.s1.at[block, k - 1], self.r1.at[block, k - 1], self.along(block, 0, k),
        )

    def first_start(self, block):
        for k in (2, 1, 3):
            self.first_copy(block, k).start()

    def first_end(self, block):
        mine = self.axes(block)[0]
        for k in range(1, 4):
            self.first_copy(block, k).wait()
        own = self.pair[block, pl.ds(pl.multiple_of(mine * 288, 32), 288)]
        got = [self.got1[block, k].astype(jnp.float32) for k in range(3)]
        self.part2[block] = (own + got[0]) + (got[1] + got[2])

    def second_copy(self, block, k):
        mine = self.axes(block)[1]
        rows = pl.ds(pl.multiple_of(lax.rem(mine + k, 4) * 72, 8), 72)
        return self.copy(
            self.part2.at[block, rows], self.got2.at[block, k - 1],
            self.s2.at[block, k - 1], self.r2.at[block, k - 1], self.along(block, 1, k),
        )

    def second_start(self, block):
        for k in (2, 1, 3):
            self.second_copy(block, k).start()

    def second_end(self, block):
        mine = self.axes(block)[1]
        half, odd = block // 2, block % 2
        for k in range(1, 4):
            self.second_copy(block, k).wait()
        own = self.part2[block, pl.ds(pl.multiple_of(mine * 72, 8), 72)]
        total = (own + self.got2[block, 0]) + (self.got2[block, 1] + self.got2[block, 2])
        for other in range(8):
            self.ztx[half, other, 8 * odd : 8 * odd + 8] = total[8 * other : 8 * other + 8]
            if other % 2 == odd:
                self.ztx[half, other, 16:24] = total[64:72]

    def z_copy(self, half, k):
        core, x, y, z = self.spot
        other = lax.rem(z + k, 8)
        return self.copy(
            self.ztx.at[half, other], self.zrx.at[half, z], self.zs.at[half, k - 1], self.zr.at[half, k - 1],
            device(core, x, y, other),
        )

    def z_start(self, half):
        z = self.spot[3]
        for k in (4, 3, 5, 2, 6, 1, 7):
            self.z_copy(half, k).start()
        self.zrx[half, z] = self.ztx[half, z]

    def z_end(self, half):
        core, x, y, z = self.spot
        for k in range(1, 8):
            self.z_copy(half, k).wait_send()
            origin = lax.rem(z + 8 - k, 8)
            self.copy(
                self.ztx.at[half, z], self.zrx.at[half, origin], self.zs.at[half, k - 1], self.zr.at[half, k - 1],
                device(core, x, y, origin),
            ).wait_recv()
        total = self.zrx[half, 0]
        for other in range(1, 8):
            total = total + self.zrx[half, other]
        tile = total[16:24]
        rest = tile - tile.astype(jnp.bfloat16).astype(jnp.float32)
        odd = lax.rem(z, 2)
        one, two = (1 - odd) * x + odd * y, (1 - odd) * y + odd * x
        row = lax.broadcasted_iota(jnp.int32, (8, 128), 0)
        index = jnp.broadcast_to(4 * one + two, (8, 128))
        moved = jnp.concatenate([rest[0:2], rest[0:2], rest[0:4]], axis=0)
        tile = jnp.where((index == 14) & (row >= 2) & (row < 4), moved, tile)
        self.gtx[half] = jnp.concatenate([total[0:16], tile, jnp.zeros((8, 128), jnp.float32)], axis=0).astype(
            jnp.bfloat16
        )

    def gather_z_copy(self, half, k, spot_z):
        core, x, y, z = self.spot
        return self.copy(
            self.gtx.at[half], self.zall.at[half, spot_z], self.gz_s.at[half, k - 1], self.gz_r.at[half, k - 1],
            device(core, x, y, lax.rem(z + k, 8)),
        )

    def gather_z_start(self, half):
        z = self.spot[3]
        for k in (4, 3, 5, 2, 6, 1, 7):
            self.gather_z_copy(half, k, z).start()
        self.zall[half, z] = self.gtx[half]

    def gather_z_end(self, half):
        core, _, _, z = self.spot
        for k in range(1, 8):
            self.gather_z_copy(half, k, z).wait_send()
            self.gather_z_copy(half, k, lax.rem(z + 8 - k, 8)).wait_recv()
        parts = [self.zall[half, other].astype(jnp.float32) for other in range(8)]
        for odd in range(2):
            block = 2 * half + odd
            one, two = self.axes(block)
            whole = jnp.concatenate(
                [part[8 * odd : 8 * odd + 8] for part in parts]
                + [parts[odd][16:24], jnp.zeros((8, 128), jnp.float32)],
                axis=0,
            )
            rows = pl.ds(pl.multiple_of(one * 320 + two * 80, 16), 80)
            self.out[block, core, rows] = whole.astype(jnp.bfloat16)

    def gather_copy(self, block, phase, k, sender):
        core = self.spot[0]
        one, two = self.axes(block)
        if phase == 1:
            if sender:
                two = lax.rem(two + 4 - k, 4)
            rows, size, send, recv = one * 320 + two * 80, 80, self.g2_s, self.g2_r
        else:
            if sender:
                one = lax.rem(one + 4 - k, 4)
            rows, size, send, recv = one * 320, 320, self.g1_s, self.g1_r
        spot = self.out.at[block, core, pl.ds(pl.multiple_of(rows, 16), size)]
        return self.copy(spot, spot, send.at[block, k - 1], recv.at[block, k - 1], self.along(block, phase, k))

    def gather_start(self, half, phase):
        for block in (2 * half, 2 * half + 1):
            for k in (2, 1, 3):
                self.gather_copy(block, phase, k, False).start()

    def gather_end(self, half, phase):
        for block in (2 * half, 2 * half + 1):
            for k in range(1, 4):
                self.gather_copy(block, phase, k, False).wait_send()
                self.gather_copy(block, phase, k, True).wait_recv()

    def gather_pair_copy(self, half, core_of):
        core, x, y, z = self.spot
        spot = self.out.at[pl.ds(2 * half, 2), core_of]
        return self.copy(spot, spot, self.gp_s.at[half], self.gp_r.at[half], device(1 - core, x, y, z))

    def gather_pair_start(self, half):
        self.gather_pair_copy(half, self.spot[0]).start()

    def gather_pair_end(self, half):
        self.gather_pair_copy(half, self.spot[0]).wait_send()
        self.gather_pair_copy(half, 1 - self.spot[0]).wait_recv()


def total_scratch():
    f32, bf16 = jnp.float32, jnp.bfloat16
    dma = pltpu.SemaphoreType.DMA
    buffers = [
        pltpu.VMEM((BLOCKS, 1152, 128), f32),
        pltpu.VMEM((BLOCKS, 1152, 128), WIRE),
        pltpu.VMEM((BLOCKS, 3, 288, 128), WIRE),
        pltpu.VMEM((BLOCKS, 288, 128), f32),
        pltpu.VMEM((BLOCKS, 3, 72, 128), f32),
        pltpu.VMEM((2, 8, 24, 128), f32),
        pltpu.VMEM((2, 8, 24, 128), f32),
        pltpu.VMEM((2, 32, 128), bf16),
        pltpu.VMEM((2, 8, 32, 128), bf16),
    ]
    shapes = [(BLOCKS,), (BLOCKS, 3), (BLOCKS, 3), (2, 7), (2, 7), (BLOCKS, 3), (BLOCKS, 3), (2,)]
    sems = []
    for shape in shapes:
        sems += [dma(shape), dma(shape)]
    return buffers, sems


VARS_PAD = 112
ROOT = 0.7978845608028654
CUBE = 0.044715


def chunk_rows(start, size):
    return pl.ds(pl.multiple_of(start, 128), size)


def step_kernel(
    seed, ic, target, hidden_far, table_far, w1_far, b1_far, w2_far, b2_far, bank_far, weight_far, out_far,
    out, out_sem, table, w1, b1, w2_raw, b2, bank, weight, w2, bias_out, load_sem,
    fresh_a, fresh_b, noisy, noisy_t, pre, act, pred, ens, grad_send, grad_t, part_grad, acc, *rest
):
    buffers, sems = rest[:9], rest[9:25]
    pred_s, pred_r, ret_s, ret_r = rest[25:]
    spot = place()
    core, x, y, z = spot
    z_hi, z_lo = lax.div(z, 4), lax.rem(z, 4)
    me = y * 4 + z_lo
    others = [(t, i) for t in range(4) for i in range(4) if t + i > 0]

    def member_at(t, i):
        return lax.rem(y + t, 4) * 4 + lax.rem(z_lo + i, 4)

    def member_device(member):
        return (lax.axis_index("cuts"), member, x)

    known = [member_device(member_at(t, i)) for t, i in others]
    known += [device(1 - core, x, y, z)]
    known += [device(core, lax.rem(x + k, 4), y, z) for k in range(1, 4)]
    known += [device(core, x, y, (1 - z_hi) * 4 + k) for k in range(4)]
    def load(t):
        rows = chunk_rows(lax.rem(y + t, 4) * 512, 512)
        return pltpu.make_async_copy(hidden_far.at[rows], noisy.at[rows], load_sem.at[t])

    pairs = [(table_far, table), (w1_far, w1), (b1_far, b1), (w2_far, w2_raw), (b2_far, b2), (bank_far, bank),
             (weight_far, weight)]
    loads = [pltpu.make_async_copy(far, near, load_sem.at[4 + n]) for n, (far, near) in enumerate(pairs)]
    load_table, load_w1, load_b1, load_w2, load_b2, load_bank, load_weight = loads
    load_table.start()
    load(0).start()
    for one in loads[1:]:
        one.start()
    for t in range(1, 4):
        load(t).start()
    load_w2.wait()
    load_b2.wait()
    w2[...] = jnp.zeros_like(w2)
    w2[0:100] = w2_raw[...]
    bias_out[...] = jnp.zeros_like(bias_out)
    bias_out[:, 0:100] = b2[...]
    wide_bias = jnp.broadcast_to(bias_out[...], (VARS_PAD, 128))
    lane = lax.broadcasted_iota(jnp.int32, (VARS_PAD, 128), 1)
    line = lax.broadcasted_iota(jnp.int32, (VARS_PAD, 128), 0)
    bias_column = jnp.sum(jnp.where(lane == line, wide_bias, 0.0), axis=1, keepdims=True)
    greet(known)
    load_table.wait()

    def pred_copy(t, i, source):
        owner = member_at(t, i)
        slot = 4 * t + i - 1
        return pltpu.make_async_remote_copy(
            src_ref=pred.at[owner, 0:104], dst_ref=ens.at[source, 0:104],
            send_sem=pred_s.at[slot], recv_sem=pred_r.at[slot],
            device_id=member_device(owner), device_id_type=MESH,
        )

    def back_copy(t, i, source):
        owner = member_at(t, i)
        slot = 4 * t + i - 1
        return pltpu.make_async_remote_copy(
            src_ref=grad_send.at[owner], dst_ref=grad_t.at[:, chunk_rows(source * 128, 128)],
            send_sem=ret_s.at[slot], recv_sem=ret_r.at[slot],
            device_id=member_device(owner), device_id_type=MESH,
        )

    def source_of(t, i):
        return lax.rem(y + 4 - t, 4) * 4 + lax.rem(z_lo + 4 - i, 4)

    fresh = (fresh_a, fresh_b)
    noise = table[pl.ds(seed[0], 1), :]

    for t in range(4):
        top = lax.rem(y + t, 4) * 512

        load(t).wait()

        def add_noise(q, _):
            rows = chunk_rows(top + q * 128, 128)
            noisy[rows, :] = (noisy[rows, :].astype(jnp.float32) + noise).astype(jnp.bfloat16)
            return 0

        lax.fori_loop(0, 4, add_noise, 0)
        rows = chunk_rows(top, 512)
        if t == 0:
            load_w1.wait()
            load_b1.wait()

        for n in range(5):
            if n < 4:
                fresh[n % 2][...] = jnp.dot(
                    noisy[rows, :], w1[:, 256 * n : 256 * n + 256], preferred_element_type=jnp.float32
                )
            if n > 0:
                columns = slice(256 * n - 256, 256 * n)
                bias = b1[:, columns]
                for strip in range(16):
                    here = pl.ds(pl.multiple_of(top + 32 * strip, 32), 32)
                    v = fresh[(n - 1) % 2][32 * strip : 32 * strip + 32] + bias
                    pre[here, columns] = v
                    bend = jnp.tanh(v * (ROOT + (ROOT * CUBE) * (v * v)))
                    half = 0.5 * v
                    act[here, columns] = (half + half * bend).astype(jnp.bfloat16)
        guess = lax.dot_general(
            w2[...], act[rows, :], (((1,), (1,)), ((), ())), preferred_element_type=jnp.float32
        ) + bias_column
        base = lax.rem(y + t, 4) * 4
        for i in range(4):
            pred[base + i] = guess[:, 128 * i : 128 * i + 128]
        for i in range(4):
            if t + i > 0:
                pred_copy(t, i, me).start()
    ens[me] = pred[me]

    def bend_back(r, _):
        rows = chunk_rows(r * 128, 128)

        def piece(n, _):
            columns = chunk_rows(n * 256, 256)
            v = pre[rows, columns]
            square = v * v
            bend = jnp.tanh(v * (ROOT + (ROOT * CUBE) * square))
            slope = ROOT + (3.0 * ROOT * CUBE) * square
            pre[rows, columns] = 0.5 * ((1.0 + bend) + (v * slope) * (1.0 - bend * bend))
            return 0

        lax.fori_loop(0, 4, piece, 0)
        return 0

    lax.fori_loop(0, 16, bend_back, 0)

    def turn(r, _):
        rows = chunk_rows(r * 256, 256)

        def piece(n, _):
            columns = chunk_rows(n * 256, 256)
            noisy_t[columns, rows] = noisy[rows, columns].T
            return 0

        lax.fori_loop(0, 4, piece, 0)
        return 0

    lax.fori_loop(0, 8, turn, 0)

    for t, i in others:
        pred_copy(t, i, me).wait_send()
        pred_copy(t, i, source_of(t, i)).wait_recv()

    epsilon = (1.0 - FAIR_ALPHA) / 16
    pair_scale = (1.0 - epsilon) / (16 * 15.0)
    load_bank.wait()
    load_weight.wait()
    area = weight[...]

    def score(start, size):
        rows = pl.ds(start, size)
        first = bank[ic[0], rows, 0, 0, :]
        truth = bank[target[0], rows, 0, 0, :]
        values = [ens[m, rows, :] + first for m in range(16)]
        ranks = [None] * 16
        for a in range(16):
            for b in range(a + 1, 16):
                low = values[a] < values[b]
                high = values[a] > values[b]
                sign = jnp.where(high, 1.0, jnp.where(low, -1.0, 0.0))
                ranks[a] = sign if ranks[a] is None else ranks[a] + sign
                ranks[b] = -sign if ranks[b] is None else ranks[b] - sign
        skill = jnp.zeros((size, 128), jnp.float32)
        spread = jnp.zeros((size, 128), jnp.float32)
        for m in range(16):
            error = values[m] - truth
            skill = skill + jnp.abs(error)
            spread = spread + error * ranks[m]
            side = jnp.where(values[m] > truth, 1.0, jnp.where(values[m] < truth, -1.0, 0.0))
            ens[m, rows, :] = (area / 4) * (side / 16 - pair_scale * ranks[m])
        return area * (skill / 16 - pair_scale * spread)

    def score_step(s, total):
        return total + score(pl.multiple_of(s * 8, 8), 8)

    total = lax.fori_loop(0, 12, score_step, jnp.zeros((8, 128), jnp.float32))
    total = jnp.sum(total, axis=0, keepdims=True) + jnp.sum(score(96, 4), axis=0, keepdims=True)
    total = total / (4.0 * 8192 * 100)

    inside = lax.broadcasted_iota(jnp.int32, (VARS_PAD, 128), 0) < 100
    for t, i in [(0, 0)] + others:
        owner = member_at(t, i)
        value = jnp.where(inside, ens[owner], 0.0).astype(jnp.bfloat16)
        if t + i > 0:
            grad_send[owner] = value
            back_copy(t, i, me).start()
        else:
            grad_t[:, chunk_rows(me * 128, 128)] = value
    for t, i in others:
        back_copy(t, i, me).wait_send()
        back_copy(t, i, source_of(t, i)).wait_recv()

    job = Total(spot, acc, out, *buffers, sems)
    ones = jnp.ones((16, 2048), jnp.bfloat16)
    bias_row = lax.dot_general(
        ones, grad_t[...], (((1,), (1,)), ((), ())), preferred_element_type=jnp.float32
    )[0:1]
    bias_row = jnp.concatenate([bias_row, jnp.zeros((1, 16), jnp.float32)], axis=1)

    def packed_row(r):
        return (r // 32) * 288 + (r % 32) // 8 * 72 + 64

    def backward(block):
        columns = pl.ds(block * 256, 256)

        def spread_back(r, bias):
            rows = chunk_rows(r * 512, 512)
            carried = lax.dot_general(
                grad_t[:, rows], w2[:, columns], (((0,), (0,)), ((), ())), preferred_element_type=jnp.float32
            )
            value = (carried * pre[rows, columns]).astype(jnp.bfloat16)
            part_grad[rows, :] = value
            return bias + jnp.sum(value.astype(jnp.float32), axis=0, keepdims=True)

        bias = lax.fori_loop(0, 4, spread_back, jnp.zeros((1, 256), jnp.float32))

        wide = jnp.dot(noisy_t[...], part_grad[...], preferred_element_type=jnp.float32)
        for c in range(16):
            start = (c // 4) * 288 + (c % 4) * 72
            acc[start : start + 64, columns] = wide[64 * c : 64 * c + 64]
        second = jnp.dot(grad_t[...], act[:, columns], preferred_element_type=jnp.float32)
        for r in range(0, VARS_PAD, 8):
            acc[pl.ds(packed_row(r), 8), columns] = second[r : r + 8]
        row = packed_row(112)
        acc[pl.ds(row, 8), columns] = jnp.zeros((8, 256), jnp.float32)
        acc[pl.ds(packed_row(120), 8), columns] = jnp.zeros((8, 256), jnp.float32)
        acc[pl.ds(row, 1), columns] = bias
        if block == 0:
            acc[pl.ds(row + 1, 1), pl.ds(0, 128)] = bias_row
            acc[pl.ds(row + 1, 1), pl.ds(128, 128)] = total

    for block in range(BLOCKS):
        backward(block)
        job.pair_start(block)
        if block >= 1:
            job.pair_end(block - 1)
            job.first_start(block - 1)
        if block >= 2:
            job.first_end(block - 2)
            job.second_start(block - 2)
        if block >= 3:
            job.second_end(block - 3)
    job.pair_end(3)
    job.first_start(3)
    job.second_end(1)
    job.z_start(0)
    job.first_end(2)
    job.second_start(2)
    job.first_end(3)
    job.second_start(3)
    job.z_end(0)
    job.gather_z_start(0)
    job.second_end(2)
    job.second_end(3)
    job.z_start(1)
    job.gather_z_end(0)
    job.gather_start(0, 1)
    job.z_end(1)
    job.gather_z_start(1)
    job.gather_end(0, 1)
    job.gather_start(0, 0)
    job.gather_z_end(1)
    job.gather_start(1, 1)
    job.gather_end(0, 0)
    job.gather_pair_start(0)
    job.gather_end(1, 1)
    job.gather_start(1, 0)
    job.gather_pair_end(0)
    first = pl.ds(0, 2)
    stores = [pltpu.make_async_copy(out.at[first], out_far.at[first], out_sem.at[0])]
    stores[0].start()
    job.gather_end(1, 0)
    job.gather_pair_start(1)
    last = pl.ds(2, 2)
    stores += [pltpu.make_async_copy(out.at[last, core], out_far.at[last, core], out_sem.at[1])]
    stores[1].start()
    job.gather_pair_end(1)
    stores += [pltpu.make_async_copy(out.at[last, 1 - core], out_far.at[last, 1 - core], out_sem.at[2])]
    stores[2].start()
    for one in stores:
        one.wait()


def final_kernel(summed_far, grad_w1, grad_b1, grad_w2, grad_b2, loss, summed, wide, sem, load_sem):
    copies = []
    loads = []
    for c in range(4):
        rows = pl.ds(320 * c, 320)
        loads.append(pltpu.make_async_copy(summed_far.at[:, :, rows], summed.at[:, :, rows], load_sem.at[c]))
        loads[-1].start()
    for q in range(16):
        if q % 4 == 0:
            loads[q // 4].wait()
        for block in range(BLOCKS):
            for core in range(2):
                column = slice(block * 256 + core * 128, block * 256 + core * 128 + 128)
                tile = summed[block, core, 80 * q : 80 * q + 80].astype(jnp.float32)
                wide[64 * q : 64 * q + 64, column] = tile[0:64]
                if q < 12:
                    grad_w2[8 * q : 8 * q + 8, column] = tile[64:72]
                elif q == 12:
                    grad_w2[96:100, column] = tile[64:68]
                elif q == 14:
                    grad_b1[:, column] = tile[64:65] + tile[66:67]
                    if block == 0 and core == 0:
                        grad_b2[...] = (tile[65:66] + tile[67:68])[:, 0:100]
                    if block == 0 and core == 1:
                        loss[...] = jnp.sum(tile[65:66] + tile[67:68], axis=1, keepdims=True)
        if q % 2 == 1:
            rows = pl.ds(64 * (q - 1), 128)
            copies.append(pltpu.make_async_copy(wide.at[rows], grad_w1.at[rows], sem.at[q // 2]))
            copies[-1].start()
    for one in copies:
        one.wait()


def finish(summed):
    f32 = jnp.float32
    vmem = pl.BlockSpec(memory_space=pltpu.VMEM)
    far = pl.BlockSpec(memory_space=pltpu.HBM)
    shapes = [(1024, 1024), (1, 1024), (100, 1024), (1, 100), (1, 1)]
    return pl.pallas_call(
        final_kernel,
        out_shape=[jax.ShapeDtypeStruct(s, f32) for s in shapes],
        in_specs=[far],
        out_specs=[far] + [vmem] * 4,
        scratch_shapes=[
            pltpu.VMEM((BLOCKS, 2, 1280, 128), jnp.bfloat16),
            pltpu.VMEM((1024, 1024), f32),
            pltpu.SemaphoreType.DMA((8,)),
            pltpu.SemaphoreType.DMA((4,)),
        ],
        compiler_params=pltpu.CompilerParams(vmem_limit_bytes=60 * 1024 * 1024),
    )(summed)


def whole_step(seed, ic, target, *arrays):
    total_buffers, total_sems = total_scratch()
    bf16, f32 = jnp.bfloat16, jnp.float32
    dma = pltpu.SemaphoreType.DMA
    far = pl.BlockSpec(memory_space=pltpu.HBM)
    smem = pl.BlockSpec(memory_space=pltpu.SMEM)
    return pl.pallas_call(
        step_kernel,
        out_shape=jax.ShapeDtypeStruct((BLOCKS, 2, 1280, 128), bf16),
        in_specs=[smem] * 3 + [far] * 8,
        out_specs=far,
        scratch_shapes=[
            pltpu.VMEM((BLOCKS, 2, 1280, 128), bf16),
            dma((3,)),
            pltpu.VMEM((64, 1024), f32),
            pltpu.VMEM((1024, 1024), bf16),
            pltpu.VMEM((1, 1024), f32),
            pltpu.VMEM((100, 1024), bf16),
            pltpu.VMEM((1, 100), f32),
            pltpu.VMEM((8, 100, 1, 1, 128), f32),
            pltpu.VMEM((1, 128), f32),
            pltpu.VMEM((VARS_PAD, 1024), bf16),
            pltpu.VMEM((1, 128), f32),
            dma((11,)),
            pltpu.VMEM((512, 256), f32),
            pltpu.VMEM((512, 256), f32),
            pltpu.VMEM((2048, 1024), bf16),
            pltpu.VMEM((1024, 2048), bf16),
            pltpu.VMEM((2048, 1024), f32),
            pltpu.VMEM((2048, 1024), bf16),
            pltpu.VMEM((16, VARS_PAD, 128), f32),
            pltpu.VMEM((16, VARS_PAD, 128), f32),
            pltpu.VMEM((16, VARS_PAD, 128), bf16),
            pltpu.VMEM((VARS_PAD, 2048), bf16),
            pltpu.VMEM((2048, 256), bf16),
            pltpu.VMEM((1152, 1024), f32),
        ] + total_buffers + total_sems + [dma((15,)), dma((15,)), dma((15,)), dma((15,))],
        compiler_params=pltpu.CompilerParams(
            collective_id=0, has_side_effects=True, vmem_limit_bytes=60 * 1024 * 1024
        ),
    )(seed, ic, target, *arrays)


def body(
    hidden,
    noise_seeds,
    noise_table,
    inner_weight,
    inner_bias,
    output_weight,
    output_bias,
    state_bank,
    ic_index,
    target_index,
    area_weight,
):
    summed = whole_step(
        noise_seeds, ic_index, target_index,
        hidden.reshape(2048, 1024),
        noise_table,
        inner_weight,
        inner_bias.reshape(1, 1024),
        output_weight,
        output_bias.reshape(1, 100),
        state_bank,
        area_weight.reshape(1, 128),
    )
    grad_w1, grad_b1, grad_w2, grad_b2, loss = finish(summed)
    return grad_w1, grad_b1.reshape(1024), grad_w2, grad_b2.reshape(100), loss.reshape(())


def solution(mesh):
    return jax.shard_map(
        body,
        mesh=mesh,
        in_specs=(
            P("cuts", "member", "grid", None),
            P("member"),
            P(),
            P(),
            P(),
            P(),
            P(),
            P(None, None, "grid", "member", None),
            P("cuts"),
            P("cuts"),
            P("grid", "member", None),
        ),
        out_specs=(P(), P(), P(), P(), P()),
        check_vma=False,
    )
```

```python
import jax
import jax.numpy as jnp
from jax import lax
from jax.experimental import pallas as pl
from jax.experimental.pallas import tpu as pltpu
from jax.sharding import PartitionSpec as P

FAIR_ALPHA = 0.95
MESH = pl.DeviceIdType.MESH
BLOCKS = 4


def place():
    cuts, member, x = lax.axis_index("cuts"), lax.axis_index("member"), lax.axis_index("grid")
    core, z_hi = lax.rem(cuts, 2), lax.div(cuts, 2)
    y, z_lo = lax.div(member, 4), lax.rem(member, 4)
    return core, x, y, z_hi * 4 + z_lo


def device(core, x, y, z):
    return (lax.div(z, 4) * 2 + core, y * 4 + lax.rem(z, 4), x)


def greet(devices):
    barrier = pltpu.get_barrier_semaphore()
    for one in devices:
        pl.semaphore_signal(barrier, inc=1, device_id=one, device_id_type=MESH)
    return barrier


WIRE = jnp.bfloat16


class Total:
    def __init__(self, spot, acc, out, pair, send1, got1, part2, got2, ztx, zrx, gtx, zall, sems):
        self.spot, self.acc, self.out = spot, acc, out
        self.pair, self.send1, self.got1, self.part2, self.got2 = pair, send1, got1, part2, got2
        self.ztx, self.zrx, self.gtx, self.zall = ztx, zrx, gtx, zall
        (self.pair_s, self.pair_r, self.s1, self.r1, self.s2, self.r2, self.zs, self.zr,
         self.gz_s, self.gz_r, self.g2_s, self.g2_r, self.g1_s, self.g1_r, self.gp_s, self.gp_r) = sems

    def axes(self, block):
        _, x, y, _ = self.spot
        return (x, y) if block % 2 == 0 else (y, x)

    def along(self, block, phase, k):
        core, x, y, z = self.spot
        if (block + phase) % 2 == 0:
            return device(core, lax.rem(x + k, 4), y, z)
        return device(core, x, lax.rem(y + k, 4), z)

    def columns(self, block, core):
        return pl.ds(pl.multiple_of(block * 256 + core * 128, 128), 128)

    def copy(self, src, dst, send, recv, target):
        return pltpu.make_async_remote_copy(
            src_ref=src, dst_ref=dst, send_sem=send, recv_sem=recv, device_id=target, device_id_type=MESH
        )

    def pair_copy(self, block):
        core, x, y, z = self.spot
        return self.copy(
            self.acc.at[:, self.columns(block, 1 - core)], self.pair.at[block],
            self.pair_s.at[block], self.pair_r.at[block], device(1 - core, x, y, z),
        )

    def pair_start(self, block):
        self.pair_copy(block).start()

    def pair_end(self, block):
        columns = self.columns(block, self.spot[0])
        self.pair_copy(block).wait()

        def add(q, _):
            rows = pl.ds(pl.multiple_of(q * 288, 32), 288)
            value = self.acc[rows, columns] + self.pair[block, rows]
            self.pair[block, rows] = value
            self.send1[block, rows] = value.astype(WIRE)
            return 0

        lax.fori_loop(0, 4, add, 0)

    def first_copy(self, block, k):
        mine = self.axes(block)[0]
        rows = pl.ds(pl.multiple_of(lax.rem(mine + k, 4) * 288, 32), 288)
        return self.copy(
            self.send1.at[block, rows], self.got1.at[block, k - 1],
            self.s1.at[block, k - 1], self.r1.at[block, k - 1], self.along(block, 0, k),
        )

    def first_start(self, block):
        for k in (2, 1, 3):
            self.first_copy(block, k).start()

    def first_end(self, block):
        mine = self.axes(block)[0]
        for k in range(1, 4):
            self.first_copy(block, k).wait()
        own = self.pair[block, pl.ds(pl.multiple_of(mine * 288, 32), 288)]
        got = [self.got1[block, k].astype(jnp.float32) for k in range(3)]
        self.part2[block] = (own + got[0]) + (got[1] + got[2])

    def second_copy(self, block, k):
        mine = self.axes(block)[1]
        rows = pl.ds(pl.multiple_of(lax.rem(mine + k, 4) * 72, 8), 72)
        return self.copy(
            self.part2.at[block, rows], self.got2.at[block, k - 1],
            self.s2.at[block, k - 1], self.r2.at[block, k - 1], self.along(block, 1, k),
        )

    def second_start(self, block):
        for k in (2, 1, 3):
            self.second_copy(block, k).start()

    def second_end(self, block):
        mine = self.axes(block)[1]
        half, odd = block // 2, block % 2
        for k in range(1, 4):
            self.second_copy(block, k).wait()
        own = self.part2[block, pl.ds(pl.multiple_of(mine * 72, 8), 72)]
        total = (own + self.got2[block, 0]) + (self.got2[block, 1] + self.got2[block, 2])
        for other in range(8):
            self.ztx[half, other, 8 * odd : 8 * odd + 8] = total[8 * other : 8 * other + 8]
            if other % 2 == odd:
                self.ztx[half, other, 16:24] = total[64:72]

    def z_copy(self, half, k):
        core, x, y, z = self.spot
        other = lax.rem(z + k, 8)
        return self.copy(
            self.ztx.at[half, other], self.zrx.at[half, z], self.zs.at[half, k - 1], self.zr.at[half, k - 1],
            device(core, x, y, other),
        )

    def z_start(self, half):
        z = self.spot[3]
        for k in (4, 3, 5, 2, 6, 1, 7):
            self.z_copy(half, k).start()
        self.zrx[half, z] = self.ztx[half, z]

    def z_end(self, half):
        core, x, y, z = self.spot
        for k in range(1, 8):
            self.z_copy(half, k).wait_send()
            origin = lax.rem(z + 8 - k, 8)
            self.copy(
                self.ztx.at[half, z], self.zrx.at[half, origin], self.zs.at[half, k - 1], self.zr.at[half, k - 1],
                device(core, x, y, origin),
            ).wait_recv()
        total = self.zrx[half, 0]
        for other in range(1, 8):
            total = total + self.zrx[half, other]
        tile = total[16:24]
        rest = tile - tile.astype(jnp.bfloat16).astype(jnp.float32)
        odd = lax.rem(z, 2)
        one, two = (1 - odd) * x + odd * y, (1 - odd) * y + odd * x
        row = lax.broadcasted_iota(jnp.int32, (8, 128), 0)
        index = jnp.broadcast_to(4 * one + two, (8, 128))
        moved = jnp.concatenate([rest[0:2], rest[0:2], rest[0:4]], axis=0)
        tile = jnp.where((index == 14) & (row >= 2) & (row < 4), moved, tile)
        self.gtx[half] = jnp.concatenate([total[0:16], tile, jnp.zeros((8, 128), jnp.float32)], axis=0).astype(
            jnp.bfloat16
        )

    def gather_z_copy(self, half, k, spot_z):
        core, x, y, z = self.spot
        return self.copy(
            self.gtx.at[half], self.zall.at[half, spot_z], self.gz_s.at[half, k - 1], self.gz_r.at[half, k - 1],
            device(core, x, y, lax.rem(z + k, 8)),
        )

    def gather_z_start(self, half):
        z = self.spot[3]
        for k in (4, 3, 5, 2, 6, 1, 7):
            self.gather_z_copy(half, k, z).start()
        self.zall[half, z] = self.gtx[half]

    def gather_z_end(self, half):
        core, _, _, z = self.spot
        for k in range(1, 8):
            self.gather_z_copy(half, k, z).wait_send()
            self.gather_z_copy(half, k, lax.rem(z + 8 - k, 8)).wait_recv()
        parts = [self.zall[half, other].astype(jnp.float32) for other in range(8)]
        for odd in range(2):
            block = 2 * half + odd
            one, two = self.axes(block)
            whole = jnp.concatenate(
                [part[8 * odd : 8 * odd + 8] for part in parts]
                + [parts[odd][16:24], jnp.zeros((8, 128), jnp.float32)],
                axis=0,
            )
            rows = pl.ds(pl.multiple_of(one * 320 + two * 80, 16), 80)
            self.out[block, core, rows] = whole.astype(jnp.bfloat16)

    def gather_copy(self, block, phase, k, sender):
        core = self.spot[0]
        one, two = self.axes(block)
        if phase == 1:
            if sender:
                two = lax.rem(two + 4 - k, 4)
            rows, size, send, recv = one * 320 + two * 80, 80, self.g2_s, self.g2_r
        else:
            if sender:
                one = lax.rem(one + 4 - k, 4)
            rows, size, send, recv = one * 320, 320, self.g1_s, self.g1_r
        spot = self.out.at[block, core, pl.ds(pl.multiple_of(rows, 16), size)]
        return self.copy(spot, spot, send.at[block, k - 1], recv.at[block, k - 1], self.along(block, phase, k))

    def gather_start(self, half, phase):
        for block in (2 * half, 2 * half + 1):
            for k in (2, 1, 3):
                self.gather_copy(block, phase, k, False).start()
            if phase == 0:
                self.gather_pair_copy(block, 0, self.spot[0]).start()

    def gather_end(self, half, phase):
        for k in (1, 3, 2):
            for block in (2 * half, 2 * half + 1):
                self.gather_copy(block, phase, k, True).wait_recv()
                if phase == 0:
                    self.gather_pair_copy(block, k, self.spot[0]).start()
        for k in (1, 3, 2):
            for block in (2 * half, 2 * half + 1):
                self.gather_copy(block, phase, k, False).wait_send()

    def gather_pair_copy(self, block, k, core_of):
        core, x, y, z = self.spot
        one = lax.rem(self.axes(block)[0] + 4 - k, 4)
        spot = self.out.at[block, core_of, pl.ds(pl.multiple_of(one * 320, 16), 320)]
        return self.copy(spot, spot, self.gp_s.at[block, k], self.gp_r.at[block, k], device(1 - core, x, y, z))

    def gather_pair_end(self, half):
        for k in (0, 1, 3, 2):
            for block in (2 * half, 2 * half + 1):
                self.gather_pair_copy(block, k, self.spot[0]).wait_send()
                self.gather_pair_copy(block, k, 1 - self.spot[0]).wait_recv()


def total_scratch():
    f32, bf16 = jnp.float32, jnp.bfloat16
    dma = pltpu.SemaphoreType.DMA
    buffers = [
        pltpu.VMEM((BLOCKS, 1152, 128), f32),
        pltpu.VMEM((BLOCKS, 1152, 128), WIRE),
        pltpu.VMEM((BLOCKS, 3, 288, 128), WIRE),
        pltpu.VMEM((BLOCKS, 288, 128), f32),
        pltpu.VMEM((BLOCKS, 3, 72, 128), f32),
        pltpu.VMEM((2, 8, 24, 128), f32),
        pltpu.VMEM((2, 8, 24, 128), f32),
        pltpu.VMEM((2, 32, 128), bf16),
        pltpu.VMEM((2, 8, 32, 128), bf16),
    ]
    shapes = [(BLOCKS,), (BLOCKS, 3), (BLOCKS, 3), (2, 7), (2, 7), (BLOCKS, 3), (BLOCKS, 3), (BLOCKS, 4)]
    sems = []
    for shape in shapes:
        sems += [dma(shape), dma(shape)]
    return buffers, sems


VARS_PAD = 112
ROOT = 0.7978845608028654
CUBE = 0.044715


def chunk_rows(start, size):
    return pl.ds(pl.multiple_of(start, 128), size)


LEVELS = 31000.0


def encode(value):
    line = lax.broadcasted_iota(jnp.int32, (VARS_PAD, 128), 0)
    scale = jnp.max(jnp.abs(value), axis=0, keepdims=True) * 1.01 + 1e-30
    scale = scale.astype(jnp.bfloat16).astype(jnp.float32)
    size = jnp.floor(jnp.abs(value) * (LEVELS / scale) + 0.5)
    power = jnp.floor(size * (1.0 / 128.0))
    code = jnp.exp2(power - 125.0) * (1.0 + (size - 128.0 * power) * (1.0 / 128.0))
    code = jnp.where(value < 0.0, -code, code)
    return jnp.where(line == 104, jnp.broadcast_to(scale, (VARS_PAD, 128)), code).astype(jnp.bfloat16)


def decode(coded):
    code = coded.astype(jnp.float32)
    scale = code[104:105]
    size = jnp.abs(code)
    power = jnp.floor(jnp.log(size) * 1.4426950408889634)
    whole = jnp.floor(128.0 * (power + 124.0) + 128.0 * (size * jnp.exp2(-power)) + 0.5)
    return jnp.where(code < 0.0, -whole, whole) * (scale * (1.0 / LEVELS))


def step_kernel(
    seed, ic, target, hidden_far, table_far, w1_far, b1_far, w2_far, b2_far, bank_far, weight_far, out_far,
    out, out_sem, table, w1, b1, w2_raw, b2, bank, weight, w2, bias_out, load_sem,
    fresh_a, fresh_b, noisy_0, noisy_1, noisy_2, noisy_3, raw, noisy_t, pre, act, pred, coded, ens, grad_send, grad_t, part_a, part_b, acc, *rest
):
    buffers, sems = rest[:9], rest[9:25]
    pred_s, pred_r, ret_s, ret_r = rest[25:]
    spot = place()
    core, x, y, z = spot
    z_hi, z_lo = lax.div(z, 4), lax.rem(z, 4)
    me = y * 4 + z_lo
    others = [(t, i) for t in range(4) for i in range(4) if t + i > 0]

    def member_at(t, i):
        return lax.rem(y + t, 4) * 4 + lax.rem(z_lo + i, 4)

    def member_device(member):
        return (lax.axis_index("cuts"), member, x)

    known = [member_device(member_at(t, i)) for t, i in others]
    known += [device(1 - core, x, y, z)]
    known += [device(core, lax.rem(x + k, 4), y, z) for k in range(1, 4)]
    known += [device(core, x, y, (1 - z_hi) * 4 + k) for k in range(4)]
    barrier = greet(known)

    def load(t):
        rows = chunk_rows(lax.rem(y + t, 4) * 512, 512)
        return pltpu.make_async_copy(hidden_far.at[rows], raw.at[pl.ds(512 * t, 512)], load_sem.at[t])

    pairs = [(table_far, table), (w1_far, w1), (b1_far, b1), (w2_far, w2_raw), (b2_far, b2), (bank_far.at[:, :, 0, 0, :], bank),
             (weight_far, weight)]
    loads = [pltpu.make_async_copy(far, near, load_sem.at[4 + n]) for n, (far, near) in enumerate(pairs)]
    load_table, load_w1, load_b1, load_w2, load_b2, load_bank, load_weight = loads
    load_table.start()
    load(0).start()
    for one in loads[1:]:
        one.start()
    for t in range(1, 4):
        load(t).start()
    load_w2.wait()
    load_b2.wait()
    w2[...] = jnp.zeros_like(w2)
    w2[0:100] = w2_raw[...]
    bias_out[...] = jnp.zeros_like(bias_out)
    bias_out[:, 0:100] = b2[...]
    wide_bias = jnp.broadcast_to(bias_out[...], (VARS_PAD, 128))
    lane = lax.broadcasted_iota(jnp.int32, (VARS_PAD, 128), 1)
    line = lax.broadcasted_iota(jnp.int32, (VARS_PAD, 128), 0)
    bias_column = jnp.sum(jnp.where(lane == line, wide_bias, 0.0), axis=1, keepdims=True)
    load_table.wait()

    def pred_copy(t, i, source):
        owner = member_at(t, i)
        slot = 4 * t + i - 1
        return pltpu.make_async_remote_copy(
            src_ref=pred.at[4 * t + lax.rem(z_lo + i, 4)], dst_ref=coded.at[source],
            send_sem=pred_s.at[slot], recv_sem=pred_r.at[slot],
            device_id=member_device(owner), device_id_type=MESH,
        )

    def back_copy(t, i, column):
        owner = member_at(t, i)
        slot = 4 * t + i - 1
        return pltpu.make_async_remote_copy(
            src_ref=grad_send.at[owner], dst_ref=grad_t.at[:, chunk_rows((4 - t) % 4 * 512 + column * 128, 128)],
            send_sem=ret_s.at[slot], recv_sem=ret_r.at[slot],
            device_id=member_device(owner), device_id_type=MESH,
        )

    def source_of(t, i):
        return lax.rem(y + 4 - t, 4) * 4 + lax.rem(z_lo + 4 - i, 4)

    fresh = (fresh_a, fresh_b)
    noisy = (noisy_0, noisy_1, noisy_2, noisy_3)
    parts = (part_a, part_b)
    noise = table[pl.ds(seed[0], 1), :]

    def add_noise(t, q):
        for strip in range(8):
            start = 128 * q + 16 * strip
            value = raw[512 * t + start : 512 * t + start + 16].astype(jnp.float32) + noise
            noisy[t][start : start + 16] = value.astype(jnp.bfloat16)

    load(0).wait()
    for q in range(4):
        add_noise(0, q)

    for t in range(4):
        top = 512 * t
        if t < 3:
            load(t + 1).wait()
        if t == 0:
            load_w1.wait()
            load_b1.wait()
        for n in range(5):
            if n < 4:
                fresh[n % 2][...] = jnp.dot(
                    noisy[t][...], w1[:, 256 * n : 256 * n + 256], preferred_element_type=jnp.float32
                )
                if t < 3:
                    add_noise(t + 1, n)
            if n > 0:
                columns = slice(256 * n - 256, 256 * n)
                bias = b1[:, columns]
                for strip in range(16):
                    here = slice(top + 32 * strip, top + 32 * strip + 32)
                    v = fresh[(n - 1) % 2][32 * strip : 32 * strip + 32] + bias
                    pre[here, columns] = v
                    bend = jnp.tanh(v * (ROOT + (ROOT * CUBE) * (v * v)))
                    half = 0.5 * v
                    act[here, columns] = (half + half * bend).astype(jnp.bfloat16)
        guess = lax.dot_general(
            w2[...], act[top : top + 512], (((1,), (1,)), ((), ())), preferred_element_type=jnp.float32
        )
        for i in range(4):
            pred[4 * t + i] = encode(guess[:, 128 * i : 128 * i + 128])
        if t == 0:
            pl.semaphore_wait(barrier, len(known))
        for i in range(4):
            if t + i > 0:
                pred_copy(t, i, me).start()
    coded[me] = pred[z_lo]

    def bend_back(r, _):
        rows = chunk_rows(r * 128, 128)

        def piece(n, _):
            columns = chunk_rows(n * 256, 256)
            v = pre[rows, columns]
            square = v * v
            bend = jnp.tanh(v * (ROOT + (ROOT * CUBE) * square))
            slope = ROOT + (3.0 * ROOT * CUBE) * square
            pre[rows, columns] = 0.5 * ((1.0 + bend) + (v * slope) * (1.0 - bend * bend))
            return 0

        lax.fori_loop(0, 4, piece, 0)
        return 0

    lax.fori_loop(0, 16, bend_back, 0)

    for t in range(4):

        def turn(n, _):
            columns = chunk_rows(n * 256, 256)
            for r in range(2):
                start = 512 * t + 256 * r
                noisy_t[columns, start : start + 256] = noisy[t][256 * r : 256 * r + 256, columns].T
            return 0

        lax.fori_loop(0, 4, turn, 0)
    noisy_t[1024:1040] = jnp.ones((16, 2048), jnp.bfloat16)

    for t, i in others:
        pred_copy(t, i, me).wait_send()
        pred_copy(t, i, source_of(t, i)).wait_recv()

    def open_member(m, _):
        ens[m] = decode(coded[m]) + bias_column
        return 0

    lax.fori_loop(0, 16, open_member, 0)
    epsilon = (1.0 - FAIR_ALPHA) / 16
    pair_scale = (1.0 - epsilon) / (16 * 15.0)
    load_bank.wait()
    load_weight.wait()
    area = weight[...]

    def score(start, size):
        rows = pl.ds(start, size)
        first = bank[ic[0], rows, :]
        truth = bank[target[0], rows, :]
        values = [ens[m, rows, :] + first for m in range(16)]
        ranks = [None] * 16
        for a in range(16):
            for b in range(a + 1, 16):
                low = values[a] < values[b]
                high = values[a] > values[b]
                sign = jnp.where(high, 1.0, jnp.where(low, -1.0, 0.0))
                ranks[a] = sign if ranks[a] is None else ranks[a] + sign
                ranks[b] = -sign if ranks[b] is None else ranks[b] - sign
        skill = jnp.zeros((size, 128), jnp.float32)
        spread = jnp.zeros((size, 128), jnp.float32)
        for m in range(16):
            error = values[m] - truth
            skill = skill + jnp.abs(error)
            spread = spread + error * ranks[m]
            side = jnp.where(values[m] > truth, 1.0, jnp.where(values[m] < truth, -1.0, 0.0))
            ens[m, rows, :] = (area / 4) * (side / 16 - pair_scale * ranks[m])
        return area * (skill / 16 - pair_scale * spread)

    def score_step(s, total):
        return total + score(pl.multiple_of(s * 8, 8), 8)

    total = lax.fori_loop(0, 12, score_step, jnp.zeros((8, 128), jnp.float32))
    total = jnp.sum(total, axis=0, keepdims=True) + jnp.sum(score(96, 4), axis=0, keepdims=True)
    total = total / (4.0 * 8192 * 100)

    inside = lax.broadcasted_iota(jnp.int32, (VARS_PAD, 128), 0) < 100
    for t, i in [(0, 0)] + others:
        owner = member_at(t, i)
        value = jnp.where(inside, ens[owner], 0.0).astype(jnp.bfloat16)
        if t + i > 0:
            grad_send[owner] = value
            back_copy(t, i, z_lo).start()
        else:
            grad_t[:, chunk_rows(z_lo * 128, 128)] = value

    job = Total(spot, acc, out, *buffers, sems)
    def packed_row(r):
        return (r // 32) * 288 + (r % 32) // 8 * 72 + 64

    def carry(block):
        columns = slice(256 * block, 256 * block + 256)
        for r in (0, 1, 3, 2):
            if block == 0:
                t = (4 - r) % 4
                for i in range(4):
                    if t + i > 0:
                        back_copy(t, i, lax.rem(z_lo + 4 - i, 4)).wait_recv()
            carried = lax.dot_general(
                grad_t[:, 512 * r : 512 * r + 512], w2[:, columns], (((0,), (0,)), ((), ())),
                preferred_element_type=jnp.float32,
            )
            for strip in range(16):
                start = 512 * r + 32 * strip
                value = carried[32 * strip : 32 * strip + 32] * pre[start : start + 32, columns]
                parts[block % 2][start : start + 32] = value.astype(jnp.bfloat16)

    def backward(block):
        columns = slice(256 * block, 256 * block + 256)
        wide = jnp.dot(noisy_t[...], parts[block % 2][...], preferred_element_type=jnp.float32)
        for c in range(16):
            start = (c // 4) * 288 + (c % 4) * 72
            acc[start : start + 64, columns] = wide[64 * c : 64 * c + 64]
        second = jnp.dot(grad_t[...], act[:, columns], preferred_element_type=jnp.float32)
        for r in range(0, VARS_PAD, 8):
            acc[packed_row(r) : packed_row(r) + 8, columns] = second[r : r + 8]
        low = jnp.zeros((1, 256), jnp.float32)
        if block == 0:
            low = jnp.concatenate([bias_row, total], axis=1)
        row = packed_row(112)
        acc[row : row + 8, columns] = jnp.concatenate(
            [wide[1024:1025], low, jnp.zeros((6, 256), jnp.float32)], axis=0
        )
        row = packed_row(120)
        acc[row : row + 8, columns] = jnp.zeros((8, 256), jnp.float32)
        if block + 1 < BLOCKS:
            carry(block + 1)

    carry(0)
    for t, i in others:
        back_copy(t, i, z_lo).wait_send()
    ones = jnp.ones((16, 2048), jnp.bfloat16)
    bias_row = lax.dot_general(
        ones, grad_t[...], (((1,), (1,)), ((), ())), preferred_element_type=jnp.float32
    )[0:1]
    bias_row = jnp.concatenate([bias_row, jnp.zeros((1, 16), jnp.float32)], axis=1)

    first, last = pl.ds(0, 2), pl.ds(2, 2)
    store_first = pltpu.make_async_copy(out.at[first], out_far.at[first], out_sem.at[0])
    store_mine = pltpu.make_async_copy(out.at[last, core], out_far.at[last, core], out_sem.at[1])
    store_last = pltpu.make_async_copy(out.at[last, 1 - core], out_far.at[last, 1 - core], out_sem.at[2])
    for block in range(BLOCKS):
        backward(block)
        job.pair_start(block)
        if block >= 1:
            job.pair_end(block - 1)
            job.first_start(block - 1)
    job.pair_end(3)
    job.first_start(3)
    for block in range(BLOCKS):
        job.first_end(block)
        job.second_start(block)
    for half in range(2):
        job.second_end(2 * half)
        job.second_end(2 * half + 1)
        job.z_start(half)
    for half in range(2):
        job.z_end(half)
        job.gather_z_start(half)
    for half in range(2):
        job.gather_z_end(half)
        job.gather_start(half, 1)
    for half in range(2):
        job.gather_end(half, 1)
        job.gather_start(half, 0)
    job.gather_end(0, 0)
    job.gather_pair_end(0)
    store_first.start()
    job.gather_end(1, 0)
    store_mine.start()
    job.gather_pair_end(1)
    store_last.start()
    store_first.wait()
    store_mine.wait()
    store_last.wait()


def final_kernel(summed_far, grad_w1, grad_b1, grad_w2, grad_b2, loss, summed, wide, sem, load_sem):
    copies = []
    loads = []
    for c in range(4):
        rows = pl.ds(320 * c, 320)
        loads.append(pltpu.make_async_copy(summed_far.at[:, :, rows], summed.at[:, :, rows], load_sem.at[c]))
        loads[-1].start()
    for q in range(16):
        if q % 4 == 0:
            loads[q // 4].wait()
        for block in range(BLOCKS):
            for core in range(2):
                column = slice(block * 256 + core * 128, block * 256 + core * 128 + 128)
                tile = summed[block, core, 80 * q : 80 * q + 80].astype(jnp.float32)
                wide[64 * q : 64 * q + 64, column] = tile[0:64]
                if q < 12:
                    grad_w2[8 * q : 8 * q + 8, column] = tile[64:72]
                elif q == 12:
                    grad_w2[96:100, column] = tile[64:68]
                elif q == 14:
                    grad_b1[:, column] = tile[64:65] + tile[66:67]
                    if block == 0 and core == 0:
                        grad_b2[...] = (tile[65:66] + tile[67:68])[:, 0:100]
                    if block == 0 and core == 1:
                        loss[...] = jnp.sum(tile[65:66] + tile[67:68], axis=1, keepdims=True)
        if q % 2 == 1:
            rows = pl.ds(64 * (q - 1), 128)
            copies.append(pltpu.make_async_copy(wide.at[rows], grad_w1.at[rows], sem.at[q // 2]))
            copies[-1].start()
    for one in copies:
        one.wait()


def finish(summed):
    f32 = jnp.float32
    vmem = pl.BlockSpec(memory_space=pltpu.VMEM)
    far = pl.BlockSpec(memory_space=pltpu.HBM)
    shapes = [(1024, 1024), (1, 1024), (100, 1024), (1, 100), (1, 1)]
    return pl.pallas_call(
        final_kernel,
        out_shape=[jax.ShapeDtypeStruct(s, f32) for s in shapes],
        in_specs=[far],
        out_specs=[far] + [vmem] * 4,
        scratch_shapes=[
            pltpu.VMEM((BLOCKS, 2, 1280, 128), jnp.bfloat16),
            pltpu.VMEM((1024, 1024), f32),
            pltpu.SemaphoreType.DMA((8,)),
            pltpu.SemaphoreType.DMA((4,)),
        ],
        compiler_params=pltpu.CompilerParams(vmem_limit_bytes=60 * 1024 * 1024),
    )(summed)


def whole_step(seed, ic, target, *arrays):
    total_buffers, total_sems = total_scratch()
    bf16, f32 = jnp.bfloat16, jnp.float32
    dma = pltpu.SemaphoreType.DMA
    far = pl.BlockSpec(memory_space=pltpu.HBM)
    smem = pl.BlockSpec(memory_space=pltpu.SMEM)
    return pl.pallas_call(
        step_kernel,
        out_shape=jax.ShapeDtypeStruct((BLOCKS, 2, 1280, 128), bf16),
        in_specs=[smem] * 3 + [far] * 8,
        out_specs=far,
        scratch_shapes=[
            pltpu.VMEM((BLOCKS, 2, 1280, 128), bf16),
            dma((3,)),
            pltpu.VMEM((64, 1024), f32),
            pltpu.VMEM((1024, 1024), bf16),
            pltpu.VMEM((1, 1024), f32),
            pltpu.VMEM((100, 1024), bf16),
            pltpu.VMEM((1, 100), f32),
            pltpu.VMEM((8, 100, 128), f32),
            pltpu.VMEM((1, 128), f32),
            pltpu.VMEM((VARS_PAD, 1024), bf16),
            pltpu.VMEM((1, 128), f32),
            dma((11,)),
            pltpu.VMEM((512, 256), f32),
            pltpu.VMEM((512, 256), f32),
            pltpu.VMEM((512, 1024), bf16),
            pltpu.VMEM((512, 1024), bf16),
            pltpu.VMEM((512, 1024), bf16),
            pltpu.VMEM((512, 1024), bf16),
            pltpu.VMEM((2048, 1024), bf16),
            pltpu.VMEM((1040, 2048), bf16),
            pltpu.VMEM((2048, 1024), f32),
            pltpu.VMEM((2048, 1024), bf16),
            pltpu.VMEM((16, VARS_PAD, 128), bf16),
            pltpu.VMEM((16, VARS_PAD, 128), bf16),
            pltpu.VMEM((16, VARS_PAD, 128), f32),
            pltpu.VMEM((16, VARS_PAD, 128), bf16),
            pltpu.VMEM((VARS_PAD, 2048), bf16),
            pltpu.VMEM((2048, 256), bf16),
            pltpu.VMEM((2048, 256), bf16),
            pltpu.VMEM((1152, 1024), f32),
        ] + total_buffers + total_sems + [dma((15,)), dma((15,)), dma((15,)), dma((15,))],
        compiler_params=pltpu.CompilerParams(
            collective_id=0, has_side_effects=True, vmem_limit_bytes=60 * 1024 * 1024
        ),
    )(seed, ic, target, *arrays)


def body(
    hidden,
    noise_seeds,
    noise_table,
    inner_weight,
    inner_bias,
    output_weight,
    output_bias,
    state_bank,
    ic_index,
    target_index,
    area_weight,
):
    summed = whole_step(
        noise_seeds, ic_index, target_index,
        hidden.reshape(2048, 1024),
        noise_table,
        inner_weight,
        inner_bias.reshape(1, 1024),
        output_weight,
        output_bias.reshape(1, 100),
        state_bank,
        area_weight.reshape(1, 128),
    )
    grad_w1, grad_b1, grad_w2, grad_b2, loss = finish(summed)
    return grad_w1, grad_b1.reshape(1024), grad_w2, grad_b2.reshape(100), loss.reshape(())


def solution(mesh):
    return jax.shard_map(
        body,
        mesh=mesh,
        in_specs=(
            P("cuts", "member", "grid", None),
            P("member"),
            P(),
            P(),
            P(),
            P(),
            P(),
            P(None, None, "grid", "member", None),
            P("cuts"),
            P("cuts"),
            P("grid", "member", None),
        ),
        out_specs=(P(), P(), P(), P(), P()),
        check_vma=False,
    )
```

```python
import jax
import jax.numpy as jnp
from jax import lax
from jax.experimental import pallas as pl
from jax.experimental.pallas import tpu as pltpu
from jax.sharding import PartitionSpec as P

FAIR_ALPHA = 0.95
MESH = pl.DeviceIdType.MESH
BLOCKS = 4


def place():
    cuts, member, x = lax.axis_index("cuts"), lax.axis_index("member"), lax.axis_index("grid")
    core, z_hi = lax.rem(cuts, 2), lax.div(cuts, 2)
    y, z_lo = lax.div(member, 4), lax.rem(member, 4)
    return core, x, y, z_hi * 4 + z_lo


def device(core, x, y, z):
    return (lax.div(z, 4) * 2 + core, y * 4 + lax.rem(z, 4), x)


def greet(devices):
    barrier = pltpu.get_barrier_semaphore()
    for one in devices:
        pl.semaphore_signal(barrier, inc=1, device_id=one, device_id_type=MESH)
    return barrier


WIRE = jnp.bfloat16


class Total:
    def __init__(self, spot, acc, out, pair, send1, got1, part2, got2, ztx, zrx, gtx, zall, sems):
        self.spot, self.acc, self.out = spot, acc, out
        self.pair, self.send1, self.got1, self.part2, self.got2 = pair, send1, got1, part2, got2
        self.ztx, self.zrx, self.gtx, self.zall = ztx, zrx, gtx, zall
        (self.pair_s, self.pair_r, self.s1, self.r1, self.s2, self.r2, self.zs, self.zr,
         self.gz_s, self.gz_r, self.g2_s, self.g2_r, self.g1_s, self.g1_r, self.gp_s, self.gp_r) = sems

    def axes(self, block):
        _, x, y, _ = self.spot
        return (x, y) if block % 2 == 0 else (y, x)

    def along(self, block, phase, k):
        core, x, y, z = self.spot
        if (block + phase) % 2 == 0:
            return device(core, lax.rem(x + k, 4), y, z)
        return device(core, x, lax.rem(y + k, 4), z)

    def columns(self, block, core):
        return pl.ds(pl.multiple_of(block * 256 + core * 128, 128), 128)

    def copy(self, src, dst, send, recv, target):
        return pltpu.make_async_remote_copy(
            src_ref=src, dst_ref=dst, send_sem=send, recv_sem=recv, device_id=target, device_id_type=MESH
        )

    def pair_copy(self, block):
        core, x, y, z = self.spot
        return self.copy(
            self.acc.at[:, self.columns(block, 1 - core)], self.pair.at[block],
            self.pair_s.at[block], self.pair_r.at[block], device(1 - core, x, y, z),
        )

    def pair_start(self, block):
        self.pair_copy(block).start()

    def pair_end(self, block):
        columns = self.columns(block, self.spot[0])
        self.pair_copy(block).wait()

        def add(q, _):
            rows = pl.ds(pl.multiple_of(q * 288, 32), 288)
            value = self.acc[rows, columns] + self.pair[block, rows]
            self.pair[block, rows] = value
            self.send1[block, rows] = value.astype(WIRE)
            return 0

        lax.fori_loop(0, 4, add, 0)

    def first_copy(self, block, k):
        mine = self.axes(block)[0]
        rows = pl.ds(pl.multiple_of(lax.rem(mine + k, 4) * 288, 32), 288)
        return self.copy(
            self.send1.at[block, rows], self.got1.at[block, k - 1],
            self.s1.at[block, k - 1], self.r1.at[block, k - 1], self.along(block, 0, k),
        )

    def first_start(self, block):
        for k in (2, 1, 3):
            self.first_copy(block, k).start()

    def first_end(self, block):
        mine = self.axes(block)[0]
        for k in range(1, 4):
            self.first_copy(block, k).wait()
        own = self.pair[block, pl.ds(pl.multiple_of(mine * 288, 32), 288)]
        got = [self.got1[block, k].astype(jnp.float32) for k in range(3)]
        self.part2[block] = (own + got[0]) + (got[1] + got[2])

    def second_copy(self, block, k):
        mine = self.axes(block)[1]
        rows = pl.ds(pl.multiple_of(lax.rem(mine + k, 4) * 72, 8), 72)
        return self.copy(
            self.part2.at[block, rows], self.got2.at[block, k - 1],
            self.s2.at[block, k - 1], self.r2.at[block, k - 1], self.along(block, 1, k),
        )

    def second_start(self, block):
        for k in (2, 1, 3):
            self.second_copy(block, k).start()

    def second_end(self, block):
        mine = self.axes(block)[1]
        half, odd = block // 2, block % 2
        for k in range(1, 4):
            self.second_copy(block, k).wait()
        own = self.part2[block, pl.ds(pl.multiple_of(mine * 72, 8), 72)]
        total = (own + self.got2[block, 0]) + (self.got2[block, 1] + self.got2[block, 2])
        for other in range(8):
            self.ztx[half, other, 8 * odd : 8 * odd + 8] = total[8 * other : 8 * other + 8]
            if other % 2 == odd:
                self.ztx[half, other, 16:24] = total[64:72]

    def z_copy(self, half, k):
        core, x, y, z = self.spot
        other = lax.rem(z + k, 8)
        return self.copy(
            self.ztx.at[half, other], self.zrx.at[half, z], self.zs.at[half, k - 1], self.zr.at[half, k - 1],
            device(core, x, y, other),
        )

    def z_start(self, half):
        z = self.spot[3]
        for k in (4, 3, 5, 2, 6, 1, 7):
            self.z_copy(half, k).start()
        self.zrx[half, z] = self.ztx[half, z]

    def z_end(self, half):
        core, x, y, z = self.spot
        for k in range(1, 8):
            self.z_copy(half, k).wait_send()
            origin = lax.rem(z + 8 - k, 8)
            self.copy(
                self.ztx.at[half, z], self.zrx.at[half, origin], self.zs.at[half, k - 1], self.zr.at[half, k - 1],
                device(core, x, y, origin),
            ).wait_recv()
        total = self.zrx[half, 0]
        for other in range(1, 8):
            total = total + self.zrx[half, other]
        tile = total[16:24]
        rest = tile - tile.astype(jnp.bfloat16).astype(jnp.float32)
        odd = lax.rem(z, 2)
        one, two = (1 - odd) * x + odd * y, (1 - odd) * y + odd * x
        row = lax.broadcasted_iota(jnp.int32, (8, 128), 0)
        index = jnp.broadcast_to(4 * one + two, (8, 128))
        moved = jnp.concatenate([rest[0:2], rest[0:2], rest[0:4]], axis=0)
        tile = jnp.where((index == 14) & (row >= 2) & (row < 4), moved, tile)
        self.gtx[half] = jnp.concatenate([total[0:16], tile, jnp.zeros((8, 128), jnp.float32)], axis=0).astype(
            jnp.bfloat16
        )

    def gather_z_copy(self, half, k, spot_z):
        core, x, y, z = self.spot
        return self.copy(
            self.gtx.at[half], self.zall.at[half, spot_z], self.gz_s.at[half, k - 1], self.gz_r.at[half, k - 1],
            device(core, x, y, lax.rem(z + k, 8)),
        )

    def gather_z_start(self, half):
        z = self.spot[3]
        for k in (4, 3, 5, 2, 6, 1, 7):
            self.gather_z_copy(half, k, z).start()
        self.zall[half, z] = self.gtx[half]

    def gather_z_end(self, half):
        core, _, _, z = self.spot
        for k in range(1, 8):
            self.gather_z_copy(half, k, z).wait_send()
            self.gather_z_copy(half, k, lax.rem(z + 8 - k, 8)).wait_recv()
        parts = [self.zall[half, other].astype(jnp.float32) for other in range(8)]
        for odd in range(2):
            block = 2 * half + odd
            one, two = self.axes(block)
            whole = jnp.concatenate(
                [part[8 * odd : 8 * odd + 8] for part in parts]
                + [parts[odd][16:24], jnp.zeros((8, 128), jnp.float32)],
                axis=0,
            )
            rows = pl.ds(pl.multiple_of(one * 320 + two * 80, 16), 80)
            self.out[block, core, rows] = whole.astype(jnp.bfloat16)

    def gather_copy(self, block, phase, k, sender):
        core = self.spot[0]
        one, two = self.axes(block)
        if phase == 1:
            if sender:
                two = lax.rem(two + 4 - k, 4)
            rows, size, send, recv = one * 320 + two * 80, 80, self.g2_s, self.g2_r
        else:
            if sender:
                one = lax.rem(one + 4 - k, 4)
            rows, size, send, recv = one * 320, 320, self.g1_s, self.g1_r
        spot = self.out.at[block, core, pl.ds(pl.multiple_of(rows, 16), size)]
        return self.copy(spot, spot, send.at[block, k - 1], recv.at[block, k - 1], self.along(block, phase, k))

    def gather_start(self, half, phase):
        for block in (2 * half, 2 * half + 1):
            for k in (2, 1, 3):
                self.gather_copy(block, phase, k, False).start()
            if phase == 0:
                self.gather_pair_copy(block, 0, self.spot[0]).start()

    def gather_end(self, half, phase):
        for k in (1, 3, 2):
            for block in (2 * half, 2 * half + 1):
                self.gather_copy(block, phase, k, True).wait_recv()
                if phase == 0:
                    self.gather_pair_copy(block, k, self.spot[0]).start()
        for k in (1, 3, 2):
            for block in (2 * half, 2 * half + 1):
                self.gather_copy(block, phase, k, False).wait_send()

    def gather_pair_copy(self, block, k, core_of):
        core, x, y, z = self.spot
        one = lax.rem(self.axes(block)[0] + 4 - k, 4)
        spot = self.out.at[block, core_of, pl.ds(pl.multiple_of(one * 320, 16), 320)]
        return self.copy(spot, spot, self.gp_s.at[block, k], self.gp_r.at[block, k], device(1 - core, x, y, z))

    def gather_pair_end(self, half):
        for k in (0, 1, 3, 2):
            for block in (2 * half, 2 * half + 1):
                self.gather_pair_copy(block, k, self.spot[0]).wait_send()
                self.gather_pair_copy(block, k, 1 - self.spot[0]).wait_recv()


def total_scratch():
    f32, bf16 = jnp.float32, jnp.bfloat16
    dma = pltpu.SemaphoreType.DMA
    buffers = [
        pltpu.VMEM((BLOCKS, 1152, 128), f32),
        pltpu.VMEM((BLOCKS, 1152, 128), WIRE),
        pltpu.VMEM((BLOCKS, 3, 288, 128), WIRE),
        pltpu.VMEM((BLOCKS, 288, 128), f32),
        pltpu.VMEM((BLOCKS, 3, 72, 128), f32),
        pltpu.VMEM((2, 8, 24, 128), f32),
        pltpu.VMEM((2, 8, 24, 128), f32),
        pltpu.VMEM((2, 32, 128), bf16),
        pltpu.VMEM((2, 8, 32, 128), bf16),
    ]
    shapes = [(BLOCKS,), (BLOCKS, 3), (BLOCKS, 3), (2, 7), (2, 7), (BLOCKS, 3), (BLOCKS, 3), (BLOCKS, 4)]
    sems = []
    for shape in shapes:
        sems += [dma(shape), dma(shape)]
    return buffers, sems


VARS_PAD = 112
ROOT = 0.7978845608028654
CUBE = 0.044715


def chunk_rows(start, size):
    return pl.ds(pl.multiple_of(start, 128), size)


LEVELS = 31000.0


def encode(value):
    line = lax.broadcasted_iota(jnp.int32, (VARS_PAD, 128), 0)
    scale = jnp.max(jnp.abs(value), axis=0, keepdims=True) * 1.01 + 1e-30
    scale = scale.astype(jnp.bfloat16).astype(jnp.float32)
    size = jnp.floor(jnp.abs(value) * (LEVELS / scale) + 0.5)
    power = jnp.floor(size * (1.0 / 128.0))
    code = jnp.exp2(power - 125.0) * (1.0 + (size - 128.0 * power) * (1.0 / 128.0))
    code = jnp.where(value < 0.0, -code, code)
    return jnp.where(line == 104, jnp.broadcast_to(scale, (VARS_PAD, 128)), code).astype(jnp.bfloat16)


def decode(coded):
    code = coded.astype(jnp.float32)
    scale = code[104:105]
    size = jnp.abs(code)
    power = jnp.floor(jnp.log(size) * 1.4426950408889634)
    whole = jnp.floor(128.0 * (power + 124.0) + 128.0 * (size * jnp.exp2(-power)) + 0.5)
    return jnp.where(code < 0.0, -whole, whole) * (scale * (1.0 / LEVELS))


def step_kernel(
    seed, ic, target, hidden_far, table_far, w1_far, b1_far, w2_far, b2_far, bank_far, weight_far, out_far,
    out, out_sem, table, w1, b1, w2_raw, b2, bank, weight, w2, bias_out, load_sem,
    fresh_a, fresh_b, noisy_0, noisy_1, noisy_2, noisy_3, raw, noisy_t, pre, act, pred, coded, ens, grad_send, grad_t, part_a, part_b, acc, *rest
):
    buffers, sems = rest[:9], rest[9:25]
    pred_s, pred_r, ret_s, ret_r = rest[25:]
    spot = place()
    core, x, y, z = spot
    z_hi, z_lo = lax.div(z, 4), lax.rem(z, 4)
    me = y * 4 + z_lo
    others = [(t, i) for t in range(4) for i in range(4) if t + i > 0]

    def member_at(t, i):
        return lax.rem(y + t, 4) * 4 + lax.rem(z_lo + i, 4)

    def member_device(member):
        return (lax.axis_index("cuts"), member, x)

    known = [member_device(member_at(t, i)) for t, i in others]
    known += [device(1 - core, x, y, z)]
    known += [device(core, lax.rem(x + k, 4), y, z) for k in range(1, 4)]
    known += [device(core, x, y, (1 - z_hi) * 4 + k) for k in range(4)]
    barrier = greet(known)

    def load(t):
        rows = chunk_rows(lax.rem(y + t, 4) * 512, 512)
        return pltpu.make_async_copy(hidden_far.at[rows], raw.at[pl.ds(512 * t, 512)], load_sem.at[t])

    pairs = [(table_far, table), (w1_far, w1), (b1_far, b1), (w2_far, w2_raw), (b2_far, b2), (bank_far.at[:, :, 0, 0, :], bank),
             (weight_far, weight)]
    loads = [pltpu.make_async_copy(far, near, load_sem.at[4 + n]) for n, (far, near) in enumerate(pairs)]
    load_table, load_w1, load_b1, load_w2, load_b2, load_bank, load_weight = loads
    load_table.start()
    load(0).start()
    for one in loads[1:]:
        one.start()
    for t in range(1, 4):
        load(t).start()
    load_table.wait()

    def pred_copy(t, i, source):
        owner = member_at(t, i)
        slot = 4 * t + i - 1
        return pltpu.make_async_remote_copy(
            src_ref=pred.at[4 * t + lax.rem(z_lo + i, 4)], dst_ref=coded.at[source],
            send_sem=pred_s.at[slot], recv_sem=pred_r.at[slot],
            device_id=member_device(owner), device_id_type=MESH,
        )

    def back_copy(t, i, column, start, stop):
        owner = member_at(t, i)
        slot = 4 * t + i - 1
        return pltpu.make_async_remote_copy(
            src_ref=grad_send.at[owner, start:stop], dst_ref=grad_t.at[start:stop, chunk_rows((4 - t) % 4 * 512 + column * 128, 128)],
            send_sem=ret_s.at[start // 48, slot], recv_sem=ret_r.at[start // 48, slot],
            device_id=member_device(owner), device_id_type=MESH,
        )

    def source_of(t, i):
        return lax.rem(y + 4 - t, 4) * 4 + lax.rem(z_lo + 4 - i, 4)

    fresh = (fresh_a, fresh_b)
    noisy = (noisy_0, noisy_1, noisy_2, noisy_3)
    parts = (part_a, part_b)
    noise = table[pl.ds(seed[0], 1), :]

    def add_noise(t, q):
        for strip in range(8):
            start = 128 * q + 16 * strip
            value = raw[512 * t + start : 512 * t + start + 16].astype(jnp.float32) + noise
            noisy[t][start : start + 16] = value.astype(jnp.bfloat16)

    load(0).wait()
    for q in range(4):
        add_noise(0, q)

    for t in range(4):
        top = 512 * t
        if t < 3:
            load(t + 1).wait()
        if t == 0:
            load_w1.wait()
            load_b1.wait()
        for n in range(5):
            if n < 4:
                fresh[n % 2][...] = jnp.dot(
                    noisy[t][...], w1[:, 256 * n : 256 * n + 256], preferred_element_type=jnp.float32
                )
                if t < 3:
                    add_noise(t + 1, n)
            if n > 0:
                columns = slice(256 * n - 256, 256 * n)
                bias = b1[:, columns]
                for strip in range(16):
                    here = slice(top + 32 * strip, top + 32 * strip + 32)
                    v = fresh[(n - 1) % 2][32 * strip : 32 * strip + 32] + bias
                    pre[here, columns] = v
                    bend = jnp.tanh(v * (ROOT + (ROOT * CUBE) * (v * v)))
                    half = 0.5 * v
                    act[here, columns] = (half + half * bend).astype(jnp.bfloat16)
        if t == 0:
            load_w2.wait()
            w2[...] = jnp.zeros_like(w2)
            w2[0:100] = w2_raw[...]
        guess = lax.dot_general(
            w2[...], act[top : top + 512], (((1,), (1,)), ((), ())), preferred_element_type=jnp.float32
        )
        for i in range(4):
            pred[4 * t + i] = encode(guess[:, 128 * i : 128 * i + 128])
        if t == 0:
            pl.semaphore_wait(barrier, len(known))
        for i in range(4):
            if t + i > 0:
                pred_copy(t, i, me).start()
    coded[me] = pred[z_lo]
    load_b2.wait()
    bias_out[...] = jnp.zeros_like(bias_out)
    bias_out[:, 0:100] = b2[...]
    wide_bias = jnp.broadcast_to(bias_out[...], (VARS_PAD, 128))
    lane = lax.broadcasted_iota(jnp.int32, (VARS_PAD, 128), 1)
    line = lax.broadcasted_iota(jnp.int32, (VARS_PAD, 128), 0)
    bias_column = jnp.sum(jnp.where(lane == line, wide_bias, 0.0), axis=1, keepdims=True)

    def bend_back(r, _):
        rows = chunk_rows(r * 128, 128)

        def piece(n, _):
            columns = chunk_rows(n * 256, 256)
            v = pre[rows, columns]
            square = v * v
            bend = jnp.tanh(v * (ROOT + (ROOT * CUBE) * square))
            slope = ROOT + (3.0 * ROOT * CUBE) * square
            pre[rows, columns] = 0.5 * ((1.0 + bend) + (v * slope) * (1.0 - bend * bend))
            return 0

        lax.fori_loop(0, 4, piece, 0)
        return 0

    lax.fori_loop(0, 16, bend_back, 0)

    for t, i in others:
        pred_copy(t, i, me).wait_send()
        pred_copy(t, i, source_of(t, i)).wait_recv()

    def open_member(m, _):
        ens[m] = decode(coded[m]) + bias_column
        return 0

    lax.fori_loop(0, 16, open_member, 0)
    def send_back(start, stop):
        inside = lax.broadcasted_iota(jnp.int32, (stop - start, 128), 0) < 100 - start
        for t, i in [(0, 0)] + others:
            owner = member_at(t, i)
            value = jnp.where(inside, ens[owner, start:stop], 0.0).astype(jnp.bfloat16)
            if t + i > 0:
                grad_send[owner, start:stop] = value
                back_copy(t, i, z_lo, start, stop).start()
            else:
                grad_t[start:stop, chunk_rows(z_lo * 128, 128)] = value

    epsilon = (1.0 - FAIR_ALPHA) / 16
    pair_scale = (1.0 - epsilon) / (16 * 15.0)
    load_bank.wait()
    load_weight.wait()
    area = weight[...]

    def score(start, size):
        rows = pl.ds(start, size)
        first = bank[ic[0], rows, :]
        truth = bank[target[0], rows, :]
        values = [ens[m, rows, :] + first for m in range(16)]
        ranks = [None] * 16
        for a in range(16):
            for b in range(a + 1, 16):
                low = values[a] < values[b]
                high = values[a] > values[b]
                sign = jnp.where(high, 1.0, jnp.where(low, -1.0, 0.0))
                ranks[a] = sign if ranks[a] is None else ranks[a] + sign
                ranks[b] = -sign if ranks[b] is None else ranks[b] - sign
        skill = jnp.zeros((size, 128), jnp.float32)
        spread = jnp.zeros((size, 128), jnp.float32)
        for m in range(16):
            error = values[m] - truth
            skill = skill + jnp.abs(error)
            spread = spread + error * ranks[m]
            side = jnp.where(values[m] > truth, 1.0, jnp.where(values[m] < truth, -1.0, 0.0))
            ens[m, rows, :] = (area / 4) * (side / 16 - pair_scale * ranks[m])
        return area * (skill / 16 - pair_scale * spread)

    def score_step(s, total):
        return total + score(pl.multiple_of(s * 8, 8), 8)

    total = lax.fori_loop(0, 6, score_step, jnp.zeros((8, 128), jnp.float32))
    send_back(0, 48)
    total = lax.fori_loop(6, 12, score_step, total)
    total = jnp.sum(total, axis=0, keepdims=True) + jnp.sum(score(96, 4), axis=0, keepdims=True)
    total = total / (4.0 * 8192 * 100)

    send_back(48, VARS_PAD)
    for t in range(4):

        def turn(n, _):
            columns = chunk_rows(n * 256, 256)
            for r in range(2):
                start = 512 * t + 256 * r
                noisy_t[columns, start : start + 256] = noisy[t][256 * r : 256 * r + 256, columns].T
            return 0

        lax.fori_loop(0, 4, turn, 0)
    noisy_t[1024:1040] = jnp.ones((16, 2048), jnp.bfloat16)

    job = Total(spot, acc, out, *buffers, sems)
    def packed_row(r):
        return (r // 32) * 288 + (r % 32) // 8 * 72 + 64

    def carry(block):
        columns = slice(256 * block, 256 * block + 256)
        for r in (0, 1, 3, 2):
            if block == 0:
                t = (4 - r) % 4
                for i in range(4):
                    if t + i > 0:
                        back_copy(t, i, lax.rem(z_lo + 4 - i, 4), 0, 48).wait_recv()
                        back_copy(t, i, lax.rem(z_lo + 4 - i, 4), 48, VARS_PAD).wait_recv()
            carried = lax.dot_general(
                grad_t[:, 512 * r : 512 * r + 512], w2[:, columns], (((0,), (0,)), ((), ())),
                preferred_element_type=jnp.float32,
            )
            for strip in range(16):
                start = 512 * r + 32 * strip
                value = carried[32 * strip : 32 * strip + 32] * pre[start : start + 32, columns]
                parts[block % 2][start : start + 32] = value.astype(jnp.bfloat16)

    def backward(block):
        columns = slice(256 * block, 256 * block + 256)
        wide = jnp.dot(noisy_t[...], parts[block % 2][...], preferred_element_type=jnp.float32)
        for c in range(16):
            start = (c // 4) * 288 + (c % 4) * 72
            acc[start : start + 64, columns] = wide[64 * c : 64 * c + 64]
        second = jnp.dot(grad_t[...], act[:, columns], preferred_element_type=jnp.float32)
        for r in range(0, VARS_PAD, 8):
            acc[packed_row(r) : packed_row(r) + 8, columns] = second[r : r + 8]
        low = jnp.zeros((1, 256), jnp.float32)
        if block == 0:
            low = jnp.concatenate([bias_row, total], axis=1)
        row = packed_row(112)
        acc[row : row + 8, columns] = jnp.concatenate(
            [wide[1024:1025], low, jnp.zeros((6, 256), jnp.float32)], axis=0
        )
        row = packed_row(120)
        acc[row : row + 8, columns] = jnp.zeros((8, 256), jnp.float32)
        if block + 1 < BLOCKS:
            carry(block + 1)

    carry(0)
    for t, i in others:
        back_copy(t, i, z_lo, 0, 48).wait_send()
        back_copy(t, i, z_lo, 48, VARS_PAD).wait_send()
    ones = jnp.ones((16, 2048), jnp.bfloat16)
    bias_row = lax.dot_general(
        ones, grad_t[...], (((1,), (1,)), ((), ())), preferred_element_type=jnp.float32
    )[0:1]
    bias_row = jnp.concatenate([bias_row, jnp.zeros((1, 16), jnp.float32)], axis=1)

    first, last = pl.ds(0, 2), pl.ds(2, 2)
    store_first = pltpu.make_async_copy(out.at[first], out_far.at[first], out_sem.at[0])
    store_mine = pltpu.make_async_copy(out.at[last, core], out_far.at[last, core], out_sem.at[1])
    store_last = pltpu.make_async_copy(out.at[last, 1 - core], out_far.at[last, 1 - core], out_sem.at[2])
    for block in range(BLOCKS):
        backward(block)
        job.pair_start(block)
        if block >= 1:
            job.pair_end(block - 1)
            job.first_start(block - 1)
    job.pair_end(3)
    job.first_start(3)
    for block in range(BLOCKS):
        job.first_end(block)
        job.second_start(block)
    for half in range(2):
        job.second_end(2 * half)
        job.second_end(2 * half + 1)
        job.z_start(half)
    for half in range(2):
        job.z_end(half)
        job.gather_z_start(half)
    for half in range(2):
        job.gather_z_end(half)
        job.gather_start(half, 1)
    for half in range(2):
        job.gather_end(half, 1)
        job.gather_start(half, 0)
    job.gather_end(0, 0)
    job.gather_pair_end(0)
    store_first.start()
    job.gather_end(1, 0)
    store_mine.start()
    job.gather_pair_end(1)
    store_last.start()
    store_first.wait()
    store_mine.wait()
    store_last.wait()


def final_kernel(summed_far, grad_w1, grad_b1, grad_w2, grad_b2, loss, summed, wide, sem, load_sem):
    copies = []
    loads = []
    for c in range(8):
        rows = pl.ds(160 * c, 160)
        loads.append(pltpu.make_async_copy(summed_far.at[:, :, rows], summed.at[:, :, rows], load_sem.at[c]))
        loads[-1].start()
    for q in range(16):
        if q % 2 == 0:
            loads[q // 2].wait()
        for block in range(BLOCKS):
            for core in range(2):
                column = slice(block * 256 + core * 128, block * 256 + core * 128 + 128)
                tile = summed[block, core, 80 * q : 80 * q + 80].astype(jnp.float32)
                wide[64 * q : 64 * q + 64, column] = tile[0:64]
                if q < 12:
                    grad_w2[8 * q : 8 * q + 8, column] = tile[64:72]
                elif q == 12:
                    grad_w2[96:100, column] = tile[64:68]
                elif q == 14:
                    grad_b1[:, column] = tile[64:65] + tile[66:67]
                    if block == 0 and core == 0:
                        grad_b2[...] = (tile[65:66] + tile[67:68])[:, 0:100]
                    if block == 0 and core == 1:
                        loss[...] = jnp.sum(tile[65:66] + tile[67:68], axis=1, keepdims=True)
        if q % 2 == 1:
            rows = pl.ds(64 * (q - 1), 128)
            copies.append(pltpu.make_async_copy(wide.at[rows], grad_w1.at[rows], sem.at[q // 2]))
            copies[-1].start()
    for one in copies:
        one.wait()


def finish(summed):
    f32 = jnp.float32
    vmem = pl.BlockSpec(memory_space=pltpu.VMEM)
    far = pl.BlockSpec(memory_space=pltpu.HBM)
    shapes = [(1024, 1024), (1, 1024), (100, 1024), (1, 100), (1, 1)]
    return pl.pallas_call(
        final_kernel,
        out_shape=[jax.ShapeDtypeStruct(s, f32) for s in shapes],
        in_specs=[far],
        out_specs=[far] + [vmem] * 4,
        scratch_shapes=[
            pltpu.VMEM((BLOCKS, 2, 1280, 128), jnp.bfloat16),
            pltpu.VMEM((1024, 1024), f32),
            pltpu.SemaphoreType.DMA((8,)),
            pltpu.SemaphoreType.DMA((8,)),
        ],
        compiler_params=pltpu.CompilerParams(vmem_limit_bytes=60 * 1024 * 1024),
    )(summed)


def whole_step(seed, ic, target, *arrays):
    total_buffers, total_sems = total_scratch()
    bf16, f32 = jnp.bfloat16, jnp.float32
    dma = pltpu.SemaphoreType.DMA
    far = pl.BlockSpec(memory_space=pltpu.HBM)
    smem = pl.BlockSpec(memory_space=pltpu.SMEM)
    return pl.pallas_call(
        step_kernel,
        out_shape=jax.ShapeDtypeStruct((BLOCKS, 2, 1280, 128), bf16),
        in_specs=[smem] * 3 + [far] * 8,
        out_specs=far,
        scratch_shapes=[
            pltpu.VMEM((BLOCKS, 2, 1280, 128), bf16),
            dma((3,)),
            pltpu.VMEM((64, 1024), f32),
            pltpu.VMEM((1024, 1024), bf16),
            pltpu.VMEM((1, 1024), f32),
            pltpu.VMEM((100, 1024), bf16),
            pltpu.VMEM((1, 100), f32),
            pltpu.VMEM((8, 100, 128), f32),
            pltpu.VMEM((1, 128), f32),
            pltpu.VMEM((VARS_PAD, 1024), bf16),
            pltpu.VMEM((1, 128), f32),
            dma((11,)),
            pltpu.VMEM((512, 256), f32),
            pltpu.VMEM((512, 256), f32),
            pltpu.VMEM((512, 1024), bf16),
            pltpu.VMEM((512, 1024), bf16),
            pltpu.VMEM((512, 1024), bf16),
            pltpu.VMEM((512, 1024), bf16),
            pltpu.VMEM((2048, 1024), bf16),
            pltpu.VMEM((1040, 2048), bf16),
            pltpu.VMEM((2048, 1024), f32),
            pltpu.VMEM((2048, 1024), bf16),
            pltpu.VMEM((16, VARS_PAD, 128), bf16),
            pltpu.VMEM((16, VARS_PAD, 128), bf16),
            pltpu.VMEM((16, VARS_PAD, 128), f32),
            pltpu.VMEM((16, VARS_PAD, 128), bf16),
            pltpu.VMEM((VARS_PAD, 2048), bf16),
            pltpu.VMEM((2048, 256), bf16),
            pltpu.VMEM((2048, 256), bf16),
            pltpu.VMEM((1152, 1024), f32),
        ] + total_buffers + total_sems + [dma((15,)), dma((15,)), dma((2, 15)), dma((2, 15))],
        compiler_params=pltpu.CompilerParams(
            collective_id=0, has_side_effects=True, vmem_limit_bytes=60 * 1024 * 1024
        ),
    )(seed, ic, target, *arrays)


def body(
    hidden,
    noise_seeds,
    noise_table,
    inner_weight,
    inner_bias,
    output_weight,
    output_bias,
    state_bank,
    ic_index,
    target_index,
    area_weight,
):
    summed = whole_step(
        noise_seeds, ic_index, target_index,
        hidden.reshape(2048, 1024),
        noise_table,
        inner_weight,
        inner_bias.reshape(1, 1024),
        output_weight,
        output_bias.reshape(1, 100),
        state_bank,
        area_weight.reshape(1, 128),
    )
    grad_w1, grad_b1, grad_w2, grad_b2, loss = finish(summed)
    return grad_w1, grad_b1.reshape(1024), grad_w2, grad_b2.reshape(100), loss.reshape(())


def solution(mesh):
    return jax.shard_map(
        body,
        mesh=mesh,
        in_specs=(
            P("cuts", "member", "grid", None),
            P("member"),
            P(),
            P(),
            P(),
            P(),
            P(),
            P(None, None, "grid", "member", None),
            P("cuts"),
            P("cuts"),
            P("grid", "member", None),
        ),
        out_specs=(P(), P(), P(), P(), P()),
        check_vma=False,
    )
```
